768 devices in a mesh: walk: 24 (over z, x_lo), par: 32 (over x_hi, y, core).
Axes of the slice: x: 4 (x_hi: 2, x_lo: 2; x = x_hi * 2 + x_lo), y: 8, z: 12, core: 2. Of those that a mesh axis runs over, the one named last changes fastest.
Arguments:
- jacobian: float32 [3072, 16384], P('walk', 'par'), may hold values from -0.046875 to 0.046875
- coeffs: float32 [3072], P('walk'), may hold values from -0.109375 to 0.109375
Outputs:
- gram: float32 [3072, 3072], P('walk', 'par')
- update: float32 [16384], P('par')
The draws below stay inside these ranges and needn't reach their ends.
All inputs are finite; a program needn't handle non-finite values.
Results may differ from the reference program's by a relative error of at most 0.000084.
Values sent between devices are 32-bit elements; how exact they have to be, the bound alone decides.
No kernel may reach another device: no remote copies, remote signals or barrier semaphores. Data moves between devices by JAX's collectives and lax.ppermute only.
A program may use at most 32 MiB of HBM per device.

```python
import jax
import jax.numpy as jnp
from jax import lax

WALKERS = 3072
PARAMS = 16384


def steps_of(own_key, extent, shards, low, high):
    def one(axis_at, shards_of):
        draws = jax.random.uniform(jax.random.fold_in(jax.random.fold_in(own_key, 6), axis_at), (shards_of,), jnp.float32, low / len(shards), high / len(shards))
        return jnp.repeat(jnp.exp(draws), extent[axis_at] // shards_of).reshape((-1,) + (1,) * (len(extent) - axis_at - 1))

    level = one(*shards[0])
    for cut in shards[1:]:
        level = level * one(*cut)
    return level


def centred(rng, extent, spread, most, split=(), dtype=jnp.bfloat16):
    loudness = steps_of(rng, extent, split, -0.22, 0.18) if split else 1.0
    result = jax.random.normal(rng, extent, jnp.float32) * spread * loudness
    return jnp.minimum(jnp.maximum(result, -most), most).astype(dtype)


def setup_inputs(seed: int = 0) -> dict:
    key_list = jax.random.split(jax.random.key(seed), 3)
    return {
        "jacobian": centred(key_list[0], (WALKERS, PARAMS), PARAMS ** -0.5, 0.046875, ((0, 24), (1, 32)), jnp.float32),
        "coeffs": centred(key_list[1], (WALKERS,), WALKERS ** -0.5, 0.109375, ((0, 24),), jnp.float32),
    }


def reference(jacobian, coeffs):
    gram = jnp.dot(jacobian, jacobian.T, precision=lax.Precision.HIGHEST, preferred_element_type=jnp.float32)
    update = jnp.dot(coeffs, jacobian, precision=lax.Precision.HIGHEST, preferred_element_type=jnp.float32)
    return gram, update
```

```python
import numpy as np
import jax
import jax.numpy as jnp
from jax import lax
from jax.experimental import pallas as pl
from jax.experimental.pallas import tpu as pltpu
from jax.sharding import PartitionSpec as P

NZ = 12
NQ = 16
SLICE = 32
OTHER = 7

COL_OFFSET = (
    {0: 0, 1: 1, 2: 1, 3: 1, 4: 1, 5: 3, 6: 3, -1: 0, -2: 0, -3: 0, -4: -2, -5: -2},
    {0: 0, 1: 2, 2: 2, 3: 2, 4: 2, 5: 2, 6: 3, -1: 0, -2: 0, -3: 0, -4: -1, -5: -3},
)


def units_of(xl):
    units = [(c - d + 3, c + 3) for d, c in COL_OFFSET[xl].items()]
    for d in (range(-3, 3) if xl == 0 else range(-2, 4)):
        units += [(d + 3, OTHER), (OTHER, d + 3)]
    halves, counts = ([], []), [0, 0, 0]
    for unit in units:
        cls = class_of(unit[1], xl)
        halves[0 if counts[cls] < 4 else 1].append(unit)
        counts[cls] += 1
    assert len(halves[0]) == len(halves[1]) == 12
    return halves


def offset_of(block, xl):
    return (3, 1 - xl) if block == OTHER else (block - 3, xl)


def class_of(block, xl):
    d, x = offset_of(block, xl)
    return (2 * d + x) % 3


def plan():
    tables = np.zeros((3, 2, 2, 2, 12, 6), np.int32)
    pairs = [[], [], []]
    seen = set()
    for z in range(NZ):
        for xl in range(2):
            halves = units_of(xl)
            for core in range(2):
                rank = [0, 0, 0]
                for n, (row, col) in enumerate(halves[core]):
                    rd, rx = offset_of(row, xl)
                    cd, cx = offset_of(col, xl)
                    rz, cz = (z + rd) % NZ, (z + cd) % NZ
                    entry = [row, col]
                    for k in range(4):
                        index = 4 * (2 * cz + cx) + k
                        slot = index % 3
                        q = rank[slot]
                        rank[slot] += 1
                        entry.append(q * 3 + slot)
                        source = (z * 2 + xl) * 2 * NQ + q * 2 + core
                        target = (rz * 2 + rx) * 2 * NQ + index // 3
                        pairs[slot].append((source, target))
                        seen.add((target, slot))
                    for mine in range(2):
                        tables[z % 3, xl, mine, int(core != mine), n] = entry
                assert rank == [NQ, NQ, NQ]
    assert len(seen) == NZ * 2 * 2 * NQ * 3
    return tables.reshape(12, 2 * 12 * 6), pairs


def gram_kernel(table, *refs):
    blocks, keep, send, parts = refs[:8], refs[8], refs[9], refs[10]
    depth = blocks[0].shape[1]
    for b, ref in enumerate(blocks):
        value = ref[...]
        high = value.astype(jnp.bfloat16)
        parts[b, :, :depth] = high
        parts[b, :, depth:] = (value - high.astype(jnp.float32)).astype(jnp.bfloat16)
    dims = (((1,), (1,)), ((), ()))

    def dot(left, right):
        return lax.dot_general(left, right, dims, preferred_element_type=jnp.float32)

    for half, out in ((1, send), (0, keep)):
        for n in range(12):
            at = (half * 12 + n) * 6
            row, col = table[at], table[at + 1]
            row_high, row_low = parts[row, :, :depth], parts[row, :, depth:]
            col_high, col_low = parts[col, :, :depth], parts[col, :, depth:]
            tile = dot(col_high, row_high) + (dot(col_high, row_low) + dot(col_low, row_high))
            for k in range(4):
                out[table[at + 2 + k]] = tile[k * SLICE:(k + 1) * SLICE]


def gram_parts(table, blocks):
    rows, depth = blocks[0].shape
    out = jax.ShapeDtypeStruct((NQ * 3, SLICE, rows), jnp.float32)
    vmem = pl.BlockSpec(memory_space=pltpu.VMEM)
    return pl.pallas_call(
        gram_kernel,
        out_shape=(out, out),
        in_specs=[pl.BlockSpec(memory_space=pltpu.SMEM)] + [vmem] * len(blocks),
        out_specs=(vmem, vmem),
        scratch_shapes=[pltpu.VMEM((len(blocks), rows, 2 * depth), jnp.bfloat16)],
        compiler_params=pltpu.CompilerParams(vmem_limit_bytes=32 * 2**20),
    )(table, *blocks)


def walk_perm(dz, flip):
    return [
        (((z + dz) % NZ) * 2 + (x ^ flip), z * 2 + x) for z in range(NZ) for x in range(2)
    ]


def solution(mesh):
    tables, last_pairs = plan()

    def shards(jacobian, coeffs):
        walk, par = lax.axis_index("walk"), lax.axis_index("par")
        z, xl, core = walk // 2, walk % 2, par % 2
        table = lax.dynamic_index_in_dim(
            jnp.asarray(tables), ((z % 3) * 2 + xl) * 2 + core, 0, keepdims=False
        )

        def walk_get(value, dz, flip=0):
            return lax.ppermute(value, "walk", walk_perm(dz, flip))

        up1, down1 = walk_get(jacobian, 1), walk_get(jacobian, -1)
        up2, down2 = walk_get(up1, 1), walk_get(down1, -1)
        up3, down3 = walk_get(up2, 1), walk_get(down2, -1)
        other = walk_get(up2, 1, 1)

        term = jnp.sum(coeffs[:, None] * jacobian, axis=0)
        term = term + walk_get(term, 0, 1)
        term = term + walk_get(term, 6)
        term = term + walk_get(term, 3)
        after, before = walk_get(term, 1), walk_get(term, -1)
        place = z % 3
        first = jnp.where(place == 0, term, jnp.where(place == 1, before, after))
        second = jnp.where(place == 0, after, jnp.where(place == 1, term, before))
        third = jnp.where(place == 0, before, jnp.where(place == 1, after, term))
        update = (first + second) + third

        keep, send = gram_parts(
            table, (down3, down2, down1, jacobian, up1, up2, up3, other)
        )
        swap = [(p, p ^ 1) for p in range(2 * NQ)]
        mine = keep + lax.ppermute(send, "par", swap)
        groups = [[q * 2 + c for q in range(NQ)] for c in range(2)]
        mine = mine.reshape(NQ, 3, SLICE, -1)
        mine = lax.all_to_all(mine, "par", 0, 0, axis_index_groups=groups, tiled=True)
        mine = jnp.sum(mine, axis=0)
        slices = [
            lax.ppermute(mine[slot], ("walk", "par"), last_pairs[slot]) for slot in range(3)
        ]
        return jnp.concatenate(slices, axis=0).T, update

    in_specs = (P("walk", "par"), P("walk"))
    out_specs = (P("walk", "par"), P("par"))
    return jax.shard_map(shards, mesh=mesh, in_specs=in_specs, out_specs=out_specs, check_vma=False)
```

```python
import numpy as np
import jax
import jax.numpy as jnp
from jax import lax
from jax.experimental import pallas as pl
from jax.experimental.pallas import tpu as pltpu
from jax.sharding import PartitionSpec as P

NZ = 12
NQ = 16
SLICE = 32
OTHER = 7

COL_OFFSET = (
    {0: 0, 1: 1, 2: 1, 3: 1, 4: 1, 5: 3, 6: 3, -1: 0, -2: 0, -3: 0, -4: -2, -5: -2},
    {0: 0, 1: 2, 2: 2, 3: 2, 4: 2, 5: 2, 6: 3, -1: 0, -2: 0, -3: 0, -4: -1, -5: -3},
)


def units_of(xl):
    units = [(c - d + 3, c + 3) for d, c in COL_OFFSET[xl].items()]
    for d in (range(-3, 3) if xl == 0 else range(-2, 4)):
        units += [(d + 3, OTHER), (OTHER, d + 3)]
    halves, counts = ([], []), [0, 0, 0]
    for unit in units:
        cls = class_of(unit[1], xl)
        halves[0 if counts[cls] < 4 else 1].append(unit)
        counts[cls] += 1
    assert len(halves[0]) == len(halves[1]) == 12
    return halves


def offset_of(block, xl):
    return (3, 1 - xl) if block == OTHER else (block - 3, xl)


def class_of(block, xl):
    d, x = offset_of(block, xl)
    return (2 * d + x) % 3


def place_of(index):
    par, slot = divmod(index, 3)
    return (slot + 2) % 3 if par % 4 == 1 else slot


def plan():
    tables = np.zeros((3, 2, 2, 2, 12, 6), np.int32)
    pairs = [[], [], []]
    seen = set()
    for z in range(NZ):
        for xl in range(2):
            halves = units_of(xl)
            for core in range(2):
                rank = [0, 0, 0]
                for n, (row, col) in enumerate(halves[core]):
                    rd, rx = offset_of(row, xl)
                    cd, cx = offset_of(col, xl)
                    rz, cz = (z + rd) % NZ, (z + cd) % NZ
                    entry = [row, col]
                    for k in range(4):
                        index = 4 * (2 * cz + cx) + k
                        slot = place_of(index)
                        q = rank[slot]
                        rank[slot] += 1
                        entry.append(q * 3 + slot)
                        source = (z * 2 + xl) * 2 * NQ + q * 2 + core
                        target = (rz * 2 + rx) * 2 * NQ + index // 3
                        pairs[slot].append((source, target))
                        seen.add((target, slot))
                    for mine in range(2):
                        tables[z % 3, xl, mine, int(core != mine), n] = entry
                assert rank == [NQ, NQ, NQ]
    assert len(seen) == NZ * 2 * 2 * NQ * 3
    assert sorted(pairs[0]) == sorted(pairs[1])
    return tables.reshape(12, 2 * 12 * 6), pairs


def gram_kernel(table, *refs):
    blocks, keep, send, parts = refs[:8], refs[8], refs[9], refs[10]
    depth = blocks[0].shape[1]
    for b, ref in enumerate(blocks):
        value = ref[...]
        high = value.astype(jnp.bfloat16)
        parts[b, :, :depth] = high
        parts[b, :, depth:] = (value - high.astype(jnp.float32)).astype(jnp.bfloat16)
    dims = (((1,), (1,)), ((), ()))

    def dot(left, right):
        return lax.dot_general(left, right, dims, preferred_element_type=jnp.float32)

    for half, out in ((1, send), (0, keep)):
        for n in range(12):
            at = (half * 12 + n) * 6
            row, col = table[at], table[at + 1]
            row_high, row_low = parts[row, :, :depth], parts[row, :, depth:]
            col_high, col_low = parts[col, :, :depth], parts[col, :, depth:]
            tile = dot(col_high, row_high) + (dot(col_high, row_low) + dot(col_low, row_high))
            for k in range(4):
                out[table[at + 2 + k]] = tile[k * SLICE:(k + 1) * SLICE]


def gram_parts(table, blocks):
    rows, depth = blocks[0].shape
    out = jax.ShapeDtypeStruct((NQ * 3, SLICE, rows), jnp.float32)
    vmem = pl.BlockSpec(memory_space=pltpu.VMEM)
    return pl.pallas_call(
        gram_kernel,
        out_shape=(out, out),
        in_specs=[pl.BlockSpec(memory_space=pltpu.SMEM)] + [vmem] * len(blocks),
        out_specs=(vmem, vmem),
        scratch_shapes=[pltpu.VMEM((len(blocks), rows, 2 * depth), jnp.bfloat16)],
        compiler_params=pltpu.CompilerParams(vmem_limit_bytes=32 * 2**20),
    )(table, *blocks)


def walk_perm(dz, flip):
    return [
        (((z + dz) % NZ) * 2 + (x ^ flip), z * 2 + x) for z in range(NZ) for x in range(2)
    ]


def solution(mesh):
    tables, (pair_perm, _, single_perm) = plan()

    def shards(jacobian, coeffs):
        walk, par = lax.axis_index("walk"), lax.axis_index("par")
        z, xl, core = walk // 2, walk % 2, par % 2
        table = lax.dynamic_index_in_dim(
            jnp.asarray(tables), ((z % 3) * 2 + xl) * 2 + core, 0, keepdims=False
        )

        def walk_get(value, dz, flip=0):
            return lax.ppermute(value, "walk", walk_perm(dz, flip))

        tie = lax.optimization_barrier

        up1, down1 = walk_get(jacobian, 1), walk_get(jacobian, -1)
        term = jnp.sum(coeffs[:, None] * jacobian, axis=0)
        up1, term = tie((up1, term + walk_get(term, 0, 1)))
        up2, down2 = walk_get(up1, 1), walk_get(down1, -1)
        up2, term = tie((up2, term + walk_get(term, 6)))
        up3, down3 = walk_get(up2, 1), walk_get(down2, -1)
        other = walk_get(up2, 1, 1)
        other, term = tie((other, term + walk_get(term, 3)))

        keep, send = gram_parts(
            table, (down3, down2, down1, jacobian, up1, up2, up3, other)
        )
        swap = [(p, p ^ 1) for p in range(2 * NQ)]
        mine = keep + lax.ppermute(send, "par", swap)
        mine, term = tie((mine, term))
        groups = [[q * 2 + c for q in range(NQ)] for c in range(2)]
        mine = mine.reshape(NQ, 3, SLICE, -1)
        mine = lax.all_to_all(mine, "par", 0, 0, axis_index_groups=groups, tiled=True)

        after, before = walk_get(term, 1), walk_get(term, -1)
        place = z % 3
        first = jnp.where(place == 0, term, jnp.where(place == 1, before, after))
        second = jnp.where(place == 0, after, jnp.where(place == 1, term, before))
        third = jnp.where(place == 0, before, jnp.where(place == 1, after, term))
        mine, update = tie((mine, (first + second) + third))

        mine = jnp.sum(mine, axis=0).reshape(3 * SLICE, -1)
        pair = lax.ppermute(mine[:2 * SLICE], ("walk", "par"), pair_perm)
        single = lax.ppermute(mine[2 * SLICE:], ("walk", "par"), single_perm)
        gram = jnp.where(
            par % 4 == 1,
            jnp.concatenate((single, pair), axis=0),
            jnp.concatenate((pair, single), axis=0),
        )
        return gram.T, update

    in_specs = (P("walk", "par"), P("walk"))
    out_specs = (P("walk", "par"), P("par"))
    return jax.shard_map(shards, mesh=mesh, in_specs=in_specs, out_specs=out_specs, check_vma=False)
```

```python
import numpy as np
import jax
import jax.numpy as jnp
from jax import lax
from jax.experimental import pallas as pl
from jax.experimental.pallas import tpu as pltpu
from jax.sharding import PartitionSpec as P

NZ = 12
NQ = 16
SLICE = 32
OTHER = 7

COL_OFFSET = (
    {0: 0, 1: 1, 2: 1, 3: 1, 4: 1, 5: 3, 6: 3, -1: 0, -2: 0, -3: 0, -4: -2, -5: -2},
    {0: 0, 1: 2, 2: 2, 3: 2, 4: 2, 5: 2, 6: 3, -1: 0, -2: 0, -3: 0, -4: -1, -5: -3},
)


def offset_of(block, xl):
    return (3, 1 - xl) if block == OTHER else (block - 3, xl)


def units_of(xl):
    units = [(c - d + 3, c + 3) for d, c in COL_OFFSET[xl].items()]
    for d in (range(-3, 3) if xl == 0 else range(-2, 4)):
        units += [(d + 3, OTHER), (OTHER, d + 3)]
    halves, counts = ([], []), [0, 0, 0]
    for unit in units:
        d, x = offset_of(unit[1], xl)
        cls = (2 * d + x) % 3
        halves[0 if counts[cls] < 4 else 1].append(unit)
        counts[cls] += 1
    assert len(halves[0]) == len(halves[1]) == 12
    return halves


def place_of(index):
    par, slot = divmod(index, 3)
    return (slot + 2) % 3 if par % 4 == 1 else slot


PLACES = tuple(tuple(place_of(4 * cls + k) for k in range(4)) for cls in range(3))


def ring_distance(a, b, n):
    return min((a - b) % n, (b - a) % n)


def distance(source, target):
    (w0, p0), (w1, p1) = source, target
    x0, x1 = (p0 // 16) * 2 + w0 % 2, (p1 // 16) * 2 + w1 % 2
    return (
        ring_distance(w0 // 2, w1 // 2, NZ)
        + ring_distance(x0, x1, 4)
        + ring_distance(p0 // 2 % 8, p1 // 2 % 8, 8)
    )


def assign(walk, core, targets):
    cost = [[distance((walk, q * 2 + core), t) ** 2 for q in range(NQ)] for t in targets]
    pick = []
    for row in cost:
        pick.append(min((q for q in range(NQ) if q not in pick), key=lambda q: row[q]))
    better = True
    while better:
        better = False
        for a in range(NQ):
            for b in range(a):
                now = cost[a][pick[a]] + cost[b][pick[b]]
                if cost[a][pick[b]] + cost[b][pick[a]] < now:
                    pick[a], pick[b] = pick[b], pick[a]
                    better = True
    return pick


def plan():
    tables = np.zeros((2 * NZ, 2, 2, 12, 6), np.int32)
    pairs = [[], [], []]
    seen = set()
    for walk in range(2 * NZ):
        z, xl = divmod(walk, 2)
        for core, half in enumerate(units_of(xl)):
            entries = []
            for row, col in half:
                rd, rx = offset_of(row, xl)
                cd, cx = offset_of(col, xl)
                entries.append(
                    (2 * ((z + cd) % NZ) + cx, 2 * ((z + rd) % NZ) + rx, row, col)
                )
            entries.sort(key=lambda e: (e[0] % 3, e[0], e[1]))
            assert [e[0] % 3 for e in entries] == [0] * 4 + [1] * 4 + [2] * 4
            slices = [
                (n, k, PLACES[e[0] % 3][k], (e[1], (4 * e[0] + k) // 3))
                for n, e in enumerate(entries)
                for k in range(4)
            ]
            table = np.zeros((12, 6), np.int32)
            for n, e in enumerate(entries):
                table[n, :2] = e[2:]
            for slot in range(3):
                chosen = [s for s in slices if s[2] == slot]
                if slot != 1:
                    picks = assign(walk, core, [s[3] for s in chosen])
                for (n, k, _, target), q in zip(chosen, picks, strict=True):
                    table[n, 2 + k] = q if slot == 2 else q * 2 + slot
                    source = walk * 2 * NQ + q * 2 + core
                    pairs[slot].append((source, target[0] * 2 * NQ + target[1]))
                    seen.add((target, slot))
            tables[walk, core, 0] = table
            tables[walk, 1 - core, 1] = table
    assert len(seen) == NZ * 2 * 2 * NQ * 3
    assert sorted(pairs[0]) == sorted(pairs[1])
    return tables.reshape(4 * NZ, 2 * 12 * 6), pairs[0], pairs[2]


def gram_kernel(table, *refs):
    blocks, outs, parts = refs[:8], refs[8:12], refs[12]
    depth = blocks[0].shape[1]
    for b, ref in enumerate(blocks):
        value = ref[...]
        high = value.astype(jnp.bfloat16)
        parts[b, :, :depth] = high
        parts[b, :, depth:] = (value - high.astype(jnp.float32)).astype(jnp.bfloat16)
    dims = (((1,), (1,)), ((), ()))

    def dot(left, right):
        return lax.dot_general(left, right, dims, preferred_element_type=jnp.float32)

    for half in (1, 0):
        for n in range(12):
            at = (half * 12 + n) * 6
            row, col = table[at], table[at + 1]
            row_high, row_low = parts[row, :, :depth], parts[row, :, depth:]
            col_high, col_low = parts[col, :, :depth], parts[col, :, depth:]
            tile = dot(col_high, row_high) + (dot(col_high, row_low) + dot(col_low, row_high))
            for k in range(4):
                out = outs[2 * half + int(PLACES[n // 4][k] == 2)]
                out[table[at + 2 + k]] = tile[k * SLICE:(k + 1) * SLICE]


def gram_parts(table, blocks):
    rows, depth = blocks[0].shape
    pairs = jax.ShapeDtypeStruct((NQ * 2, SLICE, rows), jnp.float32)
    singles = jax.ShapeDtypeStruct((NQ, SLICE, rows), jnp.float32)
    vmem = pl.BlockSpec(memory_space=pltpu.VMEM)
    return pl.pallas_call(
        gram_kernel,
        out_shape=(pairs, singles, pairs, singles),
        in_specs=[pl.BlockSpec(memory_space=pltpu.SMEM)] + [vmem] * len(blocks),
        out_specs=(vmem,) * 4,
        scratch_shapes=[pltpu.VMEM((len(blocks), rows, 2 * depth), jnp.bfloat16)],
        compiler_params=pltpu.CompilerParams(vmem_limit_bytes=32 * 2**20),
    )(table, *blocks)


def walk_perm(dz, flip):
    return [
        (((z + dz) % NZ) * 2 + (x ^ flip), z * 2 + x) for z in range(NZ) for x in range(2)
    ]


def solution(mesh):
    tables, pair_perm, single_perm = plan()
    swap = [(p, p ^ 1) for p in range(2 * NQ)]
    groups = [[q * 2 + c for q in range(NQ)] for c in range(2)]

    def shards(jacobian, coeffs):
        walk, par = lax.axis_index("walk"), lax.axis_index("par")
        table = lax.dynamic_index_in_dim(
            jnp.asarray(tables), walk * 2 + par % 2, 0, keepdims=False
        )
        tie = lax.optimization_barrier

        def walk_get(value, dz, flip=0):
            return lax.ppermute(value, "walk", walk_perm(dz, flip))

        up1, down1 = walk_get(jacobian, 1), walk_get(jacobian, -1)
        term = jnp.sum(coeffs[:, None] * jacobian, axis=0)
        up1, term = tie((up1, term + walk_get(term, 0, 1)))
        up2, down2 = walk_get(up1, 1), walk_get(down1, -1)
        up3, down3 = walk_get(up2, 1), walk_get(down2, -1)
        other = walk_get(up2, 1, 1)

        keep_pair, keep_single, send_pair, send_single = gram_parts(
            table, (down3, down2, down1, jacobian, up1, up2, up3, other)
        )
        pair = keep_pair + lax.ppermute(send_pair, "par", swap)
        single = keep_single + lax.ppermute(send_single, "par", swap)

        def across(value):
            return lax.all_to_all(value, "par", 0, 0, axis_index_groups=groups, tiled=True)

        pair, term = tie((pair, term))
        pair = across(pair.reshape(NQ, 2 * SLICE, -1))
        single = across(single)
        pair, term = tie((pair, term + walk_get(term, 6)))
        pair = lax.ppermute(jnp.sum(pair, axis=0), ("walk", "par"), pair_perm)
        single, pair, term = tie((single, pair, term + walk_get(term, 3)))
        after, before = walk_get(term, 1), walk_get(term, -1)
        place = walk // 2 % 3
        first = jnp.where(place == 0, term, jnp.where(place == 1, before, after))
        second = jnp.where(place == 0, after, jnp.where(place == 1, term, before))
        third = jnp.where(place == 0, before, jnp.where(place == 1, after, term))
        update = (first + second) + third

        single = lax.ppermute(jnp.sum(single, axis=0), ("walk", "par"), single_perm)
        gram = jnp.where(
            par % 4 == 1,
            jnp.concatenate((single, pair), axis=0),
            jnp.concatenate((pair, single), axis=0),
        )
        return gram.T, update

    in_specs = (P("walk", "par"), P("walk"))
    out_specs = (P("walk", "par"), P("par"))
    return jax.shard_map(shards, mesh=mesh, in_specs=in_specs, out_specs=out_specs, check_vma=False)
```

```python
import numpy as np
import jax
import jax.numpy as jnp
from jax import lax
from jax.experimental import pallas as pl
from jax.experimental.pallas import tpu as pltpu
from jax.sharding import PartitionSpec as P

NZ = 12
NQ = 16
SLICE = 32
OTHER = 7

COL_OFFSET = (
    {0: 0, 1: 1, 2: 1, 3: 1, 4: 1, 5: 3, 6: 3, -1: 0, -2: 0, -3: 0, -4: -2, -5: -2},
    {0: 0, 1: 2, 2: 2, 3: 2, 4: 2, 5: 2, 6: 3, -1: 0, -2: 0, -3: 0, -4: -1, -5: -3},
)


def offset_of(block, xl):
    return (3, 1 - xl) if block == OTHER else (block - 3, xl)


def units_of(xl):
    units = [(c - d + 3, c + 3) for d, c in COL_OFFSET[xl].items()]
    for d in (range(-3, 3) if xl == 0 else range(-2, 4)):
        units += [(d + 3, OTHER), (OTHER, d + 3)]
    halves, counts = ([], []), [0, 0, 0]
    for unit in units:
        d, x = offset_of(unit[1], xl)
        cls = (2 * d + x) % 3
        halves[0 if counts[cls] < 4 else 1].append(unit)
        counts[cls] += 1
    assert len(halves[0]) == len(halves[1]) == 12
    return halves


def place_of(index):
    par, slot = divmod(index, 3)
    return (slot + 2) % 3 if par % 4 == 1 else slot


def ring_distance(a, b, n):
    return min((a - b) % n, (b - a) % n)


def distance(source, target):
    (w0, p0), (w1, p1) = source, target
    x0, x1 = (p0 // 16) * 2 + w0 % 2, (p1 // 16) * 2 + w1 % 2
    return (
        ring_distance(w0 // 2, w1 // 2, NZ)
        + ring_distance(x0, x1, 4)
        + ring_distance(p0 // 2 % 8, p1 // 2 % 8, 8)
    )


def assign(walk, core, targets):
    cost = [[distance((walk, q * 2 + core), t) ** 2 for q in range(NQ)] for t in targets]
    pick = []
    for row in cost:
        pick.append(min((q for q in range(NQ) if q not in pick), key=lambda q: row[q]))
    better = True
    while better:
        better = False
        for a in range(NQ):
            for b in range(a):
                now = cost[a][pick[a]] + cost[b][pick[b]]
                if cost[a][pick[b]] + cost[b][pick[a]] < now:
                    pick[a], pick[b] = pick[b], pick[a]
                    better = True
    return pick


def plan():
    tables = np.zeros((2 * NZ, 2, 2, 12, 6), np.int32)
    pairs = [[], [], []]
    seen = set()
    for walk in range(2 * NZ):
        z, xl = divmod(walk, 2)
        for core, half in enumerate(units_of(xl)):
            entries = []
            for row, col in half:
                rd, rx = offset_of(row, xl)
                cd, cx = offset_of(col, xl)
                entries.append(
                    (2 * ((z + cd) % NZ) + cx, 2 * ((z + rd) % NZ) + rx, row, col)
                )
            slices = [
                (n, k, place_of(4 * e[0] + k), (e[1], (4 * e[0] + k) // 3))
                for n, e in enumerate(entries)
                for k in range(4)
            ]
            table = np.zeros((12, 6), np.int32)
            for n, e in enumerate(entries):
                table[n, :2] = e[2:]
            for slot in range(3):
                chosen = [s for s in slices if s[2] == slot]
                if slot != 1:
                    picks = assign(walk, core, [s[3] for s in chosen])
                for (n, k, _, target), q in zip(chosen, picks, strict=True):
                    table[n, 2 + k] = q * 3 + slot
                    source = walk * 2 * NQ + q * 2 + core
                    pairs[slot].append((source, target[0] * 2 * NQ + target[1]))
                    seen.add((target, slot))
            tables[walk, core, 0] = table
            tables[walk, 1 - core, 1] = table
    assert len(seen) == NZ * 2 * 2 * NQ * 3
    assert sorted(pairs[0]) == sorted(pairs[1])
    return tables.reshape(4 * NZ, 2 * 12 * 6), pairs[0], pairs[2]


def gram_kernel(table, *refs):
    blocks, keep, send, parts = refs[:8], refs[8], refs[9], refs[10]
    depth = blocks[0].shape[1]
    for b, ref in enumerate(blocks):
        value = ref[...]
        high = value.astype(jnp.bfloat16)
        parts[b, :, :depth] = high
        parts[b, :, depth:] = (value - high.astype(jnp.float32)).astype(jnp.bfloat16)
    dims = (((1,), (1,)), ((), ()))

    def dot(left, right):
        return lax.dot_general(left, right, dims, preferred_element_type=jnp.float32)

    for half, out in ((1, send), (0, keep)):
        for n in range(12):
            at = (half * 12 + n) * 6
            row, col = table[at], table[at + 1]
            row_high, row_low = parts[row, :, :depth], parts[row, :, depth:]
            col_high, col_low = parts[col, :, :depth], parts[col, :, depth:]
            tile = dot(col_high, row_high) + (dot(col_high, row_low) + dot(col_low, row_high))
            for k in range(4):
                out[table[at + 2 + k]] = tile[k * SLICE:(k + 1) * SLICE]


def gram_parts(table, blocks):
    rows, depth = blocks[0].shape
    out = jax.ShapeDtypeStruct((NQ * 3, SLICE, rows), jnp.float32)
    vmem = pl.BlockSpec(memory_space=pltpu.VMEM)
    return pl.pallas_call(
        gram_kernel,
        out_shape=(out, out),
        in_specs=[pl.BlockSpec(memory_space=pltpu.SMEM)] + [vmem] * len(blocks),
        out_specs=(vmem, vmem),
        scratch_shapes=[pltpu.VMEM((len(blocks), rows, 2 * depth), jnp.bfloat16)],
        compiler_params=pltpu.CompilerParams(vmem_limit_bytes=32 * 2**20),
    )(table, *blocks)


def walk_perm(dz, flip):
    return [
        (((z + dz) % NZ) * 2 + (x ^ flip), z * 2 + x) for z in range(NZ) for x in range(2)
    ]


def solution(mesh):
    tables, pair_perm, single_perm = plan()
    swap = [(p, p ^ 1) for p in range(2 * NQ)]
    groups = [[q * 2 + c for q in range(NQ)] for c in range(2)]

    def shards(jacobian, coeffs):
        walk, par = lax.axis_index("walk"), lax.axis_index("par")
        table = lax.dynamic_index_in_dim(
            jnp.asarray(tables), walk * 2 + par % 2, 0, keepdims=False
        )
        tie = lax.optimization_barrier

        def walk_get(value, dz, flip=0):
            return lax.ppermute(value, "walk", walk_perm(dz, flip))

        up1, down1 = walk_get(jacobian, 1), walk_get(jacobian, -1)
        term = jnp.sum(coeffs[:, None] * jacobian, axis=0)
        up1, term = tie((up1, term + walk_get(term, 0, 1)))
        up2, down2 = walk_get(up1, 1), walk_get(down1, -1)
        up3, down3 = walk_get(up2, 1), walk_get(down2, -1)
        other = walk_get(up2, 1, 1)

        keep, send = gram_parts(
            table, (down3, down2, down1, jacobian, up1, up2, up3, other)
        )
        mine = keep + lax.ppermute(send, "par", swap)
        mine, term = tie((mine.reshape(NQ, 3 * SLICE, -1), term))
        mine = lax.all_to_all(mine, "par", 0, 0, axis_index_groups=groups, tiled=True)

        after, before = walk_get(term, 4), walk_get(term, -4)
        place = walk // 2 // 4
        first = jnp.where(place == 0, term, jnp.where(place == 1, before, after))
        second = jnp.where(place == 0, after, jnp.where(place == 1, term, before))
        third = jnp.where(place == 0, before, jnp.where(place == 1, after, term))
        term = (first + second) + third
        update = (term + walk_get(term, 2)) + (walk_get(term, 1) + walk_get(term, -1))

        mine = jnp.sum(mine, axis=0)
        pair = lax.ppermute(mine[:2 * SLICE], ("walk", "par"), pair_perm)
        single = lax.ppermute(mine[2 * SLICE:], ("walk", "par"), single_perm)
        gram = jnp.where(
            par % 4 == 1,
            jnp.concatenate((single, pair), axis=0),
            jnp.concatenate((pair, single), axis=0),
        )
        return gram.T, update

    in_specs = (P("walk", "par"), P("walk"))
    out_specs = (P("walk", "par"), P("par"))
    return jax.shard_map(shards, mesh=mesh, in_specs=in_specs, out_specs=out_specs, check_vma=False)
```

```python
import numpy as np
import jax
import jax.numpy as jnp
from jax import lax
from jax.experimental import pallas as pl
from jax.experimental.pallas import tpu as pltpu
from jax.sharding import PartitionSpec as P

NZ = 12
NQ = 16
SLICE = 32

BLOCKS = ((0, 0), (1, 0), (2, 0), (-3, 0), (0, 1), (1, 1), (3, 0), (-3, 1))
EARLY = 6
SHARE = 12


SHARES = (
    (
        ((3, 0), (2, 3), (1, 3), (5, 3), (0, 2), (4, 2), (3, 4), (1, 1), (5, 1), (7, 2), (7, 1), (6, 1)),
        ((0, 3), (4, 3), (2, 5), (3, 2), (2, 4), (0, 1), (4, 1), (3, 1), (2, 1), (3, 6), (6, 7), (2, 7)),
    ),
    (
        ((1, 1), (5, 1), (3, 4), (3, 1), (3, 0), (2, 3), (1, 3), (1, 2), (5, 2), (3, 6), (7, 2), (6, 2)),
        ((2, 4), (5, 3), (0, 3), (4, 3), (2, 0), (0, 2), (4, 2), (3, 2), (2, 5), (7, 1), (6, 7), (2, 7)),
    ),
)


def walker_block(walk, block):
    d, e = BLOCKS[block]
    return 2 * ((walk // 2 + d) % NZ) + (walk % 2 ^ e)


def place_of(index):
    par, slot = divmod(index, 3)
    return (slot + 2) % 3 if par % 4 == 1 else slot


def ring_distance(a, b, n):
    return min((a - b) % n, (b - a) % n)


def distance(source, target):
    (w0, p0), (w1, p1) = source, target
    x0, x1 = (p0 // 16) * 2 + w0 % 2, (p1 // 16) * 2 + w1 % 2
    return (
        ring_distance(w0 // 2, w1 // 2, NZ)
        + ring_distance(x0, x1, 4)
        + ring_distance(p0 // 2 % 8, p1 // 2 % 8, 8)
    )


def assign(walk, core, targets):
    cost = [[distance((walk, q * 2 + core), t) ** 2 for q in range(NQ)] for t in targets]
    pick = []
    for row in cost:
        pick.append(min((q for q in range(NQ) if q not in pick), key=lambda q: row[q]))
    better = True
    while better:
        better = False
        for a in range(NQ):
            for b in range(a):
                now = cost[a][pick[a]] + cost[b][pick[b]]
                if cost[a][pick[b]] + cost[b][pick[a]] < now:
                    pick[a], pick[b] = pick[b], pick[a]
                    better = True
    return pick


def plan():
    tables = np.zeros((2 * NZ, 2, 2, SHARE, 6), np.int32)
    pairs = [[], [], []]
    seen = set()
    for walk in range(2 * NZ):
        for core, share in enumerate(SHARES[walk % 2]):
            entries = [
                (walker_block(walk, col), walker_block(walk, row), row, col) for row, col in share
            ]
            slices = [
                (n, k, place_of(4 * e[0] + k), (e[1], (4 * e[0] + k) // 3))
                for n, e in enumerate(entries)
                for k in range(4)
            ]
            table = np.zeros((SHARE, 6), np.int32)
            for n, e in enumerate(entries):
                table[n, :2] = e[2:]
            for slot in range(3):
                chosen = [s for s in slices if s[2] == slot]
                if slot != 1:
                    picks = assign(walk, core, [s[3] for s in chosen])
                for (n, k, _, target), q in zip(chosen, picks, strict=True):
                    table[n, 2 + k] = q * 3 + slot
                    source = walk * 2 * NQ + q * 2 + core
                    pairs[slot].append((source, target[0] * 2 * NQ + target[1]))
                    seen.add((target, slot))
            tables[walk, core, 0] = table
            tables[walk, 1 - core, 1] = table
    assert len(seen) == NZ * 2 * 2 * NQ * 3
    assert sorted(pairs[0]) == sorted(pairs[1])
    return tables.reshape(4 * NZ, 2 * SHARE * 6), pairs[0], pairs[2]


def gram_kernel(table, *refs):
    *blocks, keep, send, parts = refs
    depth = blocks[0].shape[1]
    for b, ref in enumerate(blocks):
        value = ref[...]
        high = value.astype(jnp.bfloat16)
        parts[b, :, :depth] = high
        parts[b, :, depth:] = (value - high.astype(jnp.float32)).astype(jnp.bfloat16)
    dims = (((1,), (1,)), ((), ()))

    def dot(left, right):
        return lax.dot_general(left, right, dims, preferred_element_type=jnp.float32)

    for half, out in ((1, send), (0, keep)):
        for n in range(SHARE):
            at = (half * SHARE + n) * 6
            row, col = table[at], table[at + 1]
            row_high, row_low = parts[row, :, :depth], parts[row, :, depth:]
            col_high, col_low = parts[col, :, :depth], parts[col, :, depth:]
            tile = dot(col_high, row_high) + (dot(col_high, row_low) + dot(col_low, row_high))
            for k in range(4):
                out[table[at + 2 + k]] = tile[k * SLICE:(k + 1) * SLICE]


def gram_parts(table, blocks):
    rows, depth = blocks[0].shape
    out = jax.ShapeDtypeStruct((NQ * 3, SLICE, rows), jnp.float32)
    vmem = pl.BlockSpec(memory_space=pltpu.VMEM)
    return pl.pallas_call(
        gram_kernel,
        out_shape=(out, out),
        in_specs=[pl.BlockSpec(memory_space=pltpu.SMEM)] + [vmem] * len(blocks),
        out_specs=(vmem, vmem),
        scratch_shapes=[pltpu.VMEM((len(blocks), rows, 2 * depth), jnp.bfloat16)],
        compiler_params=pltpu.CompilerParams(vmem_limit_bytes=32 * 2**20),
    )(table, *blocks)


def walk_perm(dz, flip):
    return [
        (((z + dz) % NZ) * 2 + (x ^ flip), z * 2 + x) for z in range(NZ) for x in range(2)
    ]


def solution(mesh):
    tables, pair_perm, single_perm = plan()
    swap = [(p, p ^ 1) for p in range(2 * NQ)]
    groups = [[q * 2 + c for q in range(NQ)] for c in range(2)]

    def shards(jacobian, coeffs):
        walk, par = lax.axis_index("walk"), lax.axis_index("par")
        table = lax.dynamic_index_in_dim(
            jnp.asarray(tables), walk * 2 + par % 2, 0, keepdims=False
        )
        tie = lax.optimization_barrier

        def walk_get(value, dz, flip=0):
            return lax.ppermute(value, "walk", walk_perm(dz, flip))

        down3, up2, up1 = (walk_get(jacobian, dz) for dz in (-3, 2, 1))
        pair0 = walk_get(jacobian, 0, 1)
        pair1 = walk_get(up1, 0, 1)
        up2, pair0 = tie((up2, pair0))
        down3, pair1 = tie((down3, pair1))
        pair3, up3 = walk_get(down3, 0, 1), walk_get(up2, 1)
        term = jnp.sum(coeffs[:, None] * jacobian, axis=0)
        up3, term = tie((up3, term + walk_get(term, 0, 1)))

        keep, send = gram_parts(table, (jacobian, up1, up2, down3, pair0, pair1, up3, pair3))
        mine = keep + lax.ppermute(send, "par", swap)
        mine, term = tie((mine.reshape(NQ, 3 * SLICE, -1), term))
        mine = lax.all_to_all(mine, "par", 0, 0, axis_index_groups=groups, tiled=True)

        after, before = walk_get(term, 4), walk_get(term, -4)
        place = walk // 2 // 4
        first = jnp.where(place == 0, term, jnp.where(place == 1, before, after))
        second = jnp.where(place == 0, after, jnp.where(place == 1, term, before))
        third = jnp.where(place == 0, before, jnp.where(place == 1, after, term))
        term = (first + second) + third
        update = (term + walk_get(term, 2)) + (walk_get(term, 1) + walk_get(term, -1))

        mine = jnp.sum(mine, axis=0)
        pair = lax.ppermute(mine[:2 * SLICE], ("walk", "par"), pair_perm)
        single = lax.ppermute(mine[2 * SLICE:], ("walk", "par"), single_perm)
        gram = jnp.where(
            par % 4 == 1,
            jnp.concatenate((single, pair), axis=0),
            jnp.concatenate((pair, single), axis=0),
        )
        return gram.T, update

    in_specs = (P("walk", "par"), P("walk"))
    out_specs = (P("walk", "par"), P("par"))
    return jax.shard_map(shards, mesh=mesh, in_specs=in_specs, out_specs=out_specs, check_vma=False)
```

```python
import numpy as np
import jax
import jax.numpy as jnp
from jax import lax
from jax.experimental import pallas as pl
from jax.experimental.pallas import tpu as pltpu
from jax.sharding import PartitionSpec as P

NZ = 12
NQ = 16
SLICE = 32

BLOCKS = ((0, 0), (1, 0), (2, 0), (-3, 0), (0, 1), (1, 1), (3, 0), (-3, 1))
EARLY = 6
SHARE = 12


SHARES = (
    (
        ((3, 0), (2, 3), (1, 3), (5, 3), (0, 2), (4, 2), (3, 4), (1, 1), (5, 1), (7, 2), (7, 1), (6, 1)),
        ((0, 3), (4, 3), (2, 5), (3, 2), (2, 4), (0, 1), (4, 1), (3, 1), (2, 1), (3, 6), (6, 7), (2, 7)),
    ),
    (
        ((1, 1), (5, 1), (3, 4), (3, 1), (3, 0), (2, 3), (1, 3), (1, 2), (5, 2), (3, 6), (7, 2), (6, 2)),
        ((2, 4), (5, 3), (0, 3), (4, 3), (2, 0), (0, 2), (4, 2), (3, 2), (2, 5), (7, 1), (6, 7), (2, 7)),
    ),
)


def walker_block(walk, block):
    d, e = BLOCKS[block]
    return 2 * ((walk // 2 + d) % NZ) + (walk % 2 ^ e)


def place_of(index):
    par, slot = divmod(index, 3)
    return (slot + 2) % 3 if par % 4 == 1 else slot


def ring_distance(a, b, n):
    return min((a - b) % n, (b - a) % n)


def distance(source, target):
    (w0, p0), (w1, p1) = source, target
    x0, x1 = (p0 // 16) * 2 + w0 % 2, (p1 // 16) * 2 + w1 % 2
    return (
        ring_distance(w0 // 2, w1 // 2, NZ)
        + ring_distance(x0, x1, 4)
        + ring_distance(p0 // 2 % 8, p1 // 2 % 8, 8)
    )


def assign(walk, core, targets):
    cost = [[distance((walk, q * 2 + core), t) ** 2 for q in range(NQ)] for t in targets]
    pick = []
    for row in cost:
        pick.append(min((q for q in range(NQ) if q not in pick), key=lambda q: row[q]))
    better = True
    while better:
        better = False
        for a in range(NQ):
            for b in range(a):
                now = cost[a][pick[a]] + cost[b][pick[b]]
                if cost[a][pick[b]] + cost[b][pick[a]] < now:
                    pick[a], pick[b] = pick[b], pick[a]
                    better = True
    return pick


def plan():
    tables = np.zeros((2 * NZ, 2, 2, SHARE, 6), np.int32)
    pairs = [[], [], []]
    seen = set()
    for walk in range(2 * NZ):
        for core, share in enumerate(SHARES[walk % 2]):
            entries = [
                (walker_block(walk, col), walker_block(walk, row), row, col) for row, col in share
            ]
            slices = [
                (n, k, place_of(4 * e[0] + k), (e[1], (4 * e[0] + k) // 3))
                for n, e in enumerate(entries)
                for k in range(4)
            ]
            table = np.zeros((SHARE, 6), np.int32)
            for n, e in enumerate(entries):
                table[n, :2] = e[2:]
            for slot in range(3):
                chosen = [s for s in slices if s[2] == slot]
                if slot != 1:
                    picks = assign(walk, core, [s[3] for s in chosen])
                for (n, k, _, target), q in zip(chosen, picks, strict=True):
                    table[n, 2 + k] = q * 3 + slot
                    source = walk * 2 * NQ + q * 2 + core
                    pairs[slot].append((source, target[0] * 2 * NQ + target[1]))
                    seen.add((target, slot))
            tables[walk, core, 0] = table
            tables[walk, 1 - core, 1] = table
    assert len(seen) == NZ * 2 * 2 * NQ * 3
    assert sorted(pairs[0]) == sorted(pairs[1])
    return tables.reshape(4 * NZ, 2 * SHARE * 6), pairs[0], pairs[2]


def gram_kernel(table, *refs):
    *blocks, keep, send, parts = refs
    depth = blocks[0].shape[1]
    for b, ref in enumerate(blocks):
        value = ref[...]
        high = value.astype(jnp.bfloat16)
        parts[b, :, :depth] = high
        parts[b, :, depth:] = (value - high.astype(jnp.float32)).astype(jnp.bfloat16)
    dims = (((1,), (1,)), ((), ()))

    def dot(left, right):
        return lax.dot_general(left, right, dims, preferred_element_type=jnp.float32)

    for half, out in ((1, send), (0, keep)):
        for n in range(SHARE):
            at = (half * SHARE + n) * 6
            row, col = table[at], table[at + 1]
            row_high, row_low = parts[row, :, :depth], parts[row, :, depth:]
            col_high, col_low = parts[col, :, :depth], parts[col, :, depth:]
            tile = dot(col_high, row_high) + (dot(col_high, row_low) + dot(col_low, row_high))
            for k in range(4):
                out[table[at + 2 + k]] = tile[k * SLICE:(k + 1) * SLICE]


def gram_parts(table, blocks):
    rows, depth = blocks[0].shape
    out = jax.ShapeDtypeStruct((NQ * 3, SLICE, rows), jnp.float32)
    vmem = pl.BlockSpec(memory_space=pltpu.VMEM)
    return pl.pallas_call(
        gram_kernel,
        out_shape=(out, out),
        in_specs=[pl.BlockSpec(memory_space=pltpu.SMEM)] + [vmem] * len(blocks),
        out_specs=(vmem, vmem),
        scratch_shapes=[pltpu.VMEM((len(blocks), rows, 2 * depth), jnp.bfloat16)],
        compiler_params=pltpu.CompilerParams(vmem_limit_bytes=32 * 2**20),
    )(table, *blocks)


def walk_perm(dz, flip):
    return [
        (((z + dz) % NZ) * 2 + (x ^ flip), z * 2 + x) for z in range(NZ) for x in range(2)
    ]


def solution(mesh):
    tables, pair_perm, single_perm = plan()
    swap = [(p, p ^ 1) for p in range(2 * NQ)]
    groups = [[q * 2 + c for q in range(NQ)] for c in range(2)]

    def shards(jacobian, coeffs):
        walk, par = lax.axis_index("walk"), lax.axis_index("par")
        table = lax.dynamic_index_in_dim(
            jnp.asarray(tables), walk * 2 + par % 2, 0, keepdims=False
        )
        tie = lax.optimization_barrier

        def walk_get(value, dz, flip=0):
            return lax.ppermute(value, "walk", walk_perm(dz, flip))

        down3, up2, up1 = (walk_get(jacobian, dz) for dz in (-3, 2, 1))
        pair0 = walk_get(jacobian, 0, 1)
        term = jnp.sum(coeffs[:, None] * jacobian, axis=0).reshape(1, 4, -1)
        terms = lax.all_to_all(jnp.broadcast_to(term, (2 * NZ,) + term.shape[1:]), "walk", 0, 0, tiled=True)
        pair1 = walk_get(up1, 0, 1)
        up2, pair0 = tie((up2, pair0))
        down3, pair1, terms = tie((down3, pair1, terms))
        pair3, up3 = walk_get(down3, 0, 1), walk_get(up2, 1)
        update = jnp.sum(terms, axis=0).reshape(-1)

        keep, send = gram_parts(table, (jacobian, up1, up2, down3, pair0, pair1, up3, pair3))
        mine = keep + lax.ppermute(send, "par", swap)
        mine = mine.reshape(NQ, 3 * SLICE, -1)
        mine = lax.all_to_all(mine, "par", 0, 0, axis_index_groups=groups, tiled=True)

        mine = jnp.sum(mine, axis=0)
        pair = lax.ppermute(mine[:2 * SLICE], ("walk", "par"), pair_perm)
        single = lax.ppermute(mine[2 * SLICE:], ("walk", "par"), single_perm)
        gram = jnp.where(
            par % 4 == 1,
            jnp.concatenate((single, pair), axis=0),
            jnp.concatenate((pair, single), axis=0),
        )
        return gram.T, update

    in_specs = (P("walk", "par"), P("walk"))
    out_specs = (P("walk", "par"), P("par"))
    return jax.shard_map(shards, mesh=mesh, in_specs=in_specs, out_specs=out_specs, check_vma=False)
```

```python
import functools

import numpy as np
import jax
import jax.numpy as jnp
from jax import lax
from jax.experimental import pallas as pl
from jax.experimental.pallas import tpu as pltpu
from jax.sharding import PartitionSpec as P

NZ = 12
NY = 8
NQ = 16
SLICE = 32

BLOCKS = ((0, 0), (1, 0), (2, 0), (-3, 0), (0, 1), (1, 1), (3, 0), (-3, 1))
EARLY = (0, 1, 2, 3, 4, 5)
LATE = (1, 2, 3, 6, 7)
NEARLY, NLATE = 9, 3

SHARES = (
    (
        ((3, 0), (2, 3), (1, 3), (5, 3), (0, 2), (4, 2), (3, 4), (1, 1), (5, 1), (7, 2), (7, 1), (6, 1)),
        ((0, 3), (4, 3), (2, 5), (3, 2), (2, 4), (0, 1), (4, 1), (3, 1), (2, 1), (3, 6), (6, 7), (2, 7)),
    ),
    (
        ((1, 1), (5, 1), (3, 4), (3, 1), (3, 0), (2, 3), (1, 3), (1, 2), (5, 2), (3, 6), (7, 2), (6, 2)),
        ((2, 4), (5, 3), (0, 3), (4, 3), (2, 0), (0, 2), (4, 2), (3, 2), (2, 5), (7, 1), (6, 7), (2, 7)),
    ),
)


def walker_block(walk, block):
    d, e = BLOCKS[block]
    return 2 * ((walk // 2 + d) % NZ) + (walk % 2 ^ e)


def place_of(index):
    par, slot = divmod(index, 3)
    return (slot + 2) % 3 if par % 4 == 1 else slot


def ring_distance(a, b, n):
    return min((a - b) % n, (b - a) % n)


def distance(source, target):
    (w0, p0), (w1, p1) = source, target
    x0, x1 = (p0 // 16) * 2 + w0 % 2, (p1 // 16) * 2 + w1 % 2
    return (
        ring_distance(w0 // 2, w1 // 2, NZ)
        + ring_distance(x0, x1, 4)
        + ring_distance(p0 // 2 % 8, p1 // 2 % 8, 8)
    )


def assign(walk, core, targets, late, quota):
    cost = [[distance((walk, q * 2 + core), t) ** 2 for q in range(NQ)] for t in targets]
    order = sorted(range(NQ), key=lambda n: not late[n])
    lates = sum(late)
    first = order[:quota] + order[lates:lates + NY - quota]
    pick = [0] * NQ
    for q, n in enumerate(first + [n for n in order if n not in first]):
        pick[n] = q
    better = True
    while better:
        better = False
        for a in range(NQ):
            for b in range(a):
                if late[a] != late[b] and pick[a] // NY != pick[b] // NY:
                    continue
                now = cost[a][pick[a]] + cost[b][pick[b]]
                if cost[a][pick[b]] + cost[b][pick[a]] < now:
                    pick[a], pick[b] = pick[b], pick[a]
                    better = True
    return pick


def plan():
    early_table = np.zeros((2 * NZ, 2, 2, 2, NEARLY, 6), np.int32)
    late_table = np.zeros((2 * NZ, 2, 2, 2, NLATE, 6), np.int32)
    places = np.zeros((2 * NZ, 2, 2, 2 * (NEARLY + NLATE)), np.int32)
    pairs = [[], [], []]
    seen = set()
    for walk in range(2 * NZ):
        for core, share in enumerate(SHARES[walk % 2]):
            slices = []
            for n, (row, col) in enumerate(share):
                for k in range(4):
                    index = 4 * walker_block(walk, col) + k
                    target = (walker_block(walk, row), index // 3)
                    slices.append((n, k, place_of(index), target))
            picked = {}
            quota = None
            for slot in (0, 2):
                chosen = [s for s in slices if s[2] == slot]
                late = [s[0] >= NEARLY for s in chosen]
                quota = sum(late) // 2 if slot == 0 else 2 * NLATE - 2 * quota
                for s, q in zip(chosen, assign(walk, core, [s[3] for s in chosen], late, quota)):
                    picked[s[:2]] = q
                    if slot == 0:
                        picked[s[0], s[1] + 1] = q
            rank = np.zeros((2, 2), np.int32)
            dest = {}
            for n, k, slot, target in slices:
                q = picked[n, k]
                xh, y = divmod(q, NY)
                late = int(n >= NEARLY)
                own = int(rank[late, xh])
                rank[late, xh] += 1
                dest[n, k] = xh, own
                places[walk, xh, core, late * 2 * NEARLY + own] = y * 3 + slot
                source = walk * 2 * NQ + q * 2 + core
                pairs[slot].append((source, target[0] * 2 * NQ + target[1]))
                seen.add((target, slot))
            assert (rank == [[2 * NEARLY] * 2, [2 * NLATE] * 2]).all()
            for n, (row, col) in enumerate(share):
                for xh in range(2):
                    for mine in range(2):
                        if n < NEARLY:
                            table, at, names, half = early_table, n, EARLY, 2 * NEARLY
                        else:
                            table, at, names, half = late_table, n - NEARLY, LATE, 2 * NLATE
                        entry = [names.index(row), names.index(col)]
                        for k in range(4):
                            there, own = dest[n, k]
                            entry.append(int(there != xh) * half + own)
                        table[walk, xh, mine, int(core != mine), at] = entry
    assert len(seen) == NZ * 2 * 2 * NQ * 3
    assert sorted(pairs[0]) == sorted(pairs[1])
    tables = [t.reshape(8 * NZ, -1) for t in (early_table, late_table, places)]
    return tables, pairs[0], pairs[2]


def product_kernel(count, table, *refs):
    *blocks, keep, send, parts = refs
    depth = blocks[0].shape[1]
    for b, ref in enumerate(blocks):
        value = ref[...]
        high = value.astype(jnp.bfloat16)
        parts[b, :, :depth] = high
        parts[b, :, depth:] = (value - high.astype(jnp.float32)).astype(jnp.bfloat16)
    dims = (((1,), (1,)), ((), ()))

    def dot(left, right):
        return lax.dot_general(left, right, dims, preferred_element_type=jnp.float32)

    for half, out in ((1, send), (0, keep)):
        for n in range(count):
            at = (half * count + n) * 6
            row, col = table[at], table[at + 1]
            row_high, row_low = parts[row, :, :depth], parts[row, :, depth:]
            col_high, col_low = parts[col, :, :depth], parts[col, :, depth:]
            tile = dot(col_high, row_high) + (dot(col_high, row_low) + dot(col_low, row_high))
            for k in range(4):
                out[table[at + 2 + k]] = tile[k * SLICE:(k + 1) * SLICE]


VMEM = pl.BlockSpec(memory_space=pltpu.VMEM)
SMEM = pl.BlockSpec(memory_space=pltpu.SMEM)


def products(table, count, blocks, cost):
    rows, depth = blocks[0].shape
    out = jax.ShapeDtypeStruct((4 * count, SLICE, rows), jnp.float32)
    return pl.pallas_call(
        functools.partial(product_kernel, count),
        out_shape=(out, out),
        in_specs=[SMEM] + [VMEM] * len(blocks),
        out_specs=(VMEM, VMEM),
        scratch_shapes=[pltpu.VMEM((len(blocks), rows, 2 * depth), jnp.bfloat16)],
        compiler_params=pltpu.CompilerParams(vmem_limit_bytes=32 * 2**20),
        cost_estimate=pl.CostEstimate(flops=cost, bytes_accessed=2**20, transcendentals=0),
    )(table, *blocks)


def join_kernel(places, *refs):
    *terms, out = refs
    at = 0
    for group in (terms[:3], terms[3:]):
        for n in range(group[2].shape[0]):
            out[places[at]] = group[0][n] + group[1][n] + group[2][n]
            at += 1


def join(places, early, late):
    return pl.pallas_call(
        join_kernel,
        out_shape=jax.ShapeDtypeStruct((3 * NY, SLICE, early[0].shape[2]), jnp.float32),
        in_specs=[SMEM] + [VMEM] * 6,
        out_specs=VMEM,
        compiler_params=pltpu.CompilerParams(vmem_limit_bytes=32 * 2**20),
    )(places, *early, *late)


def walk_perm(dz, flip):
    return [
        (((z + dz) % NZ) * 2 + (x ^ flip), z * 2 + x) for z in range(NZ) for x in range(2)
    ]


def solution(mesh):
    tables, pair_perm, single_perm = plan()
    core_swap = [(p, p ^ 1) for p in range(2 * NQ)]
    xh_swap = [(p, p ^ NQ) for p in range(2 * NQ)]
    along_y = [[h * NQ + y * 2 + c for y in range(NY)] for h in range(2) for c in range(2)]

    def shards(jacobian, coeffs):
        walk, par = lax.axis_index("walk"), lax.axis_index("par")
        variant = walk * 4 + par // NQ * 2 + par % 2
        early_table, late_table, places = (
            lax.dynamic_index_in_dim(jnp.asarray(t), variant, 0, keepdims=False) for t in tables
        )
        tie = lax.optimization_barrier

        def walk_get(value, dz, flip=0):
            return lax.ppermute(value, "walk", walk_perm(dz, flip))

        down3, up2, up1 = (walk_get(jacobian, dz) for dz in (-3, 2, 1))
        pair0 = walk_get(jacobian, 0, 1)
        term = jnp.sum(coeffs[:, None] * jacobian, axis=0).reshape(1, 4, -1)
        terms = lax.all_to_all(jnp.broadcast_to(term, (2 * NZ,) + term.shape[1:]), "walk", 0, 0, tiled=True)
        pair1 = walk_get(up1, 0, 1)
        up2, pair0 = tie((up2, pair0))
        down3, pair1, terms = tie((down3, pair1, terms))
        update = jnp.sum(terms, axis=0).reshape(-1)
        pair3, up3 = walk_get(down3, 0, 1), walk_get(up2, 1)

        def between(keep, send, half):
            got = lax.ppermute(send, "par", core_swap)
            away = keep[half:] + got[half:]
            return keep, got, away

        keep, send = products(early_table, NEARLY, (jacobian, up1, up2, down3, pair0, pair1), 2**28)
        keep, got, away = between(keep, send, 2 * NEARLY)
        early = (keep, got, lax.ppermute(away, "par", xh_swap))
        keep, send = products(late_table, NLATE, (up1, up2, down3, up3, pair3), 2**35)
        keep, got, away = between(keep, send, 2 * NLATE)
        late = (keep, got, lax.ppermute(away, "par", xh_swap))

        mine = join(places, early, late).reshape(NY, 3 * SLICE, -1)
        mine = lax.all_to_all(mine, "par", 0, 0, axis_index_groups=along_y, tiled=True)

        mine = jnp.sum(mine, axis=0)
        pair = lax.ppermute(mine[:2 * SLICE], ("walk", "par"), pair_perm)
        single = lax.ppermute(mine[2 * SLICE:], ("walk", "par"), single_perm)
        gram = jnp.where(
            par % 4 == 1,
            jnp.concatenate((single, pair), axis=0),
            jnp.concatenate((pair, single), axis=0),
        )
        return gram.T, update

    in_specs = (P("walk", "par"), P("walk"))
    out_specs = (P("walk", "par"), P("par"))
    return jax.shard_map(shards, mesh=mesh, in_specs=in_specs, out_specs=out_specs, check_vma=False)
```

```python
import functools

import numpy as np
import jax
import jax.numpy as jnp
from jax import lax
from jax.experimental import pallas as pl
from jax.experimental.pallas import tpu as pltpu
from jax.sharding import PartitionSpec as P

NZ = 12
NQ = 16
SLICE = 32

BLOCKS = ((0, 0), (1, 0), (2, 0), (-3, 0), (0, 1), (1, 1), (3, 0), (-3, 1))
EARLY = (0, 1, 2, 3, 4, 5)
LATE = (1, 2, 3, 6, 7)
NEARLY, NLATE, SHARE = 9, 3, 12

SHARES = (
    (
        ((3, 0), (2, 3), (1, 3), (5, 3), (0, 2), (4, 2), (3, 4), (1, 1), (5, 1), (7, 2), (7, 1), (6, 1)),
        ((0, 3), (4, 3), (2, 5), (3, 2), (2, 4), (0, 1), (4, 1), (3, 1), (2, 1), (3, 6), (6, 7), (2, 7)),
    ),
    (
        ((1, 1), (5, 1), (3, 4), (3, 1), (3, 0), (2, 3), (1, 3), (1, 2), (5, 2), (3, 6), (7, 2), (6, 2)),
        ((2, 4), (5, 3), (0, 3), (4, 3), (2, 0), (0, 2), (4, 2), (3, 2), (2, 5), (7, 1), (6, 7), (2, 7)),
    ),
)


def walker_block(walk, block):
    d, e = BLOCKS[block]
    return 2 * ((walk // 2 + d) % NZ) + (walk % 2 ^ e)


def place_of(index):
    par, slot = divmod(index, 3)
    return (slot + 2) % 3 if par % 4 == 1 else slot


def ring_distance(a, b, n):
    return min((a - b) % n, (b - a) % n)


def distance(source, target):
    (w0, p0), (w1, p1) = source, target
    x0, x1 = (p0 // 16) * 2 + w0 % 2, (p1 // 16) * 2 + w1 % 2
    return (
        ring_distance(w0 // 2, w1 // 2, NZ)
        + ring_distance(x0, x1, 4)
        + ring_distance(p0 // 2 % 8, p1 // 2 % 8, 8)
    )


def assign(walk, core, targets):
    cost = [[distance((walk, q * 2 + core), t) ** 2 for q in range(NQ)] for t in targets]
    pick = []
    for row in cost:
        pick.append(min((q for q in range(NQ) if q not in pick), key=lambda q: row[q]))
    better = True
    while better:
        better = False
        for a in range(NQ):
            for b in range(a):
                now = cost[a][pick[a]] + cost[b][pick[b]]
                if cost[a][pick[b]] + cost[b][pick[a]] < now:
                    pick[a], pick[b] = pick[b], pick[a]
                    better = True
    return pick


def held(block, core):
    return block ^ 1 if core and block in (2, 3, 6, 7) else block


def plan():
    early_table = np.zeros((2 * NZ, 2, 2, NEARLY, 2), np.int32)
    late_table = np.zeros((2 * NZ, 2, 2, NLATE, 2), np.int32)
    places = np.zeros((2 * NZ, 2, SHARE, 4), np.int32)
    pairs = [[], [], []]
    seen = set()
    for walk in range(2 * NZ):
        for core, share in enumerate(SHARES[walk % 2]):
            slices = []
            for n, (row, col) in enumerate(share):
                for k in range(4):
                    index = 4 * walker_block(walk, col) + k
                    target = (walker_block(walk, row), index // 3)
                    slices.append((n, k, place_of(index), target))
            for slot in range(3):
                chosen = [s for s in slices if s[2] == slot]
                if slot != 1:
                    picks = assign(walk, core, [s[3] for s in chosen])
                for (n, k, _, target), q in zip(chosen, picks, strict=True):
                    places[walk, core, n, k] = q * 3 + slot
                    source = walk * 2 * NQ + q * 2 + core
                    pairs[slot].append((source, target[0] * 2 * NQ + target[1]))
                    seen.add((target, slot))
            for n, (row, col) in enumerate(share):
                for mine in range(2):
                    at = [held(row, mine), held(col, mine)]
                    if n < NEARLY:
                        early_table[walk, mine, int(core != mine), n] = [EARLY.index(b) for b in at]
                    else:
                        late_table[walk, mine, int(core != mine), n - NEARLY] = [LATE.index(b) for b in at]
    assert len(seen) == NZ * 2 * 2 * NQ * 3
    assert sorted(pairs[0]) == sorted(pairs[1])
    tables = [t.reshape(4 * NZ, -1) for t in (early_table, late_table, places)]
    return np.concatenate(tables, axis=1), pairs[0], pairs[2]


def product_kernel(base, count, table, *refs):
    *blocks, keep, send, parts = refs
    depth = blocks[0].shape[1]
    for b, ref in enumerate(blocks):
        value = ref[...]
        high = value.astype(jnp.bfloat16)
        parts[b, :, :depth] = high
        parts[b, :, depth:] = (value - high.astype(jnp.float32)).astype(jnp.bfloat16)
    dims = (((1,), (1,)), ((), ()))

    def dot(left, right):
        return lax.dot_general(left, right, dims, preferred_element_type=jnp.float32)

    for half, out in ((1, send), (0, keep)):
        for n in range(count):
            at = base + (half * count + n) * 2
            row, col = table[at], table[at + 1]
            row_high, row_low = parts[row, :, :depth], parts[row, :, depth:]
            col_high, col_low = parts[col, :, :depth], parts[col, :, depth:]
            out[n] = dot(col_high, row_high) + (dot(col_high, row_low) + dot(col_low, row_high))


VMEM = pl.BlockSpec(memory_space=pltpu.VMEM)
SMEM = pl.BlockSpec(memory_space=pltpu.SMEM)


def products(table, base, count, blocks, cost):
    rows, depth = blocks[0].shape
    out = jax.ShapeDtypeStruct((count, rows, rows), jnp.float32)
    return pl.pallas_call(
        functools.partial(product_kernel, base, count),
        out_shape=(out, out),
        in_specs=[SMEM] + [VMEM] * len(blocks),
        out_specs=(VMEM, VMEM),
        scratch_shapes=[pltpu.VMEM((len(blocks), rows, 2 * depth), jnp.bfloat16)],
        compiler_params=pltpu.CompilerParams(vmem_limit_bytes=32 * 2**20),
        cost_estimate=pl.CostEstimate(flops=cost, bytes_accessed=2**20, transcendentals=0),
    )(table, *blocks)


def join_kernel(table, *refs):
    *terms, out = refs
    at = 4 * SHARE
    for kept, got in (terms[:2], terms[2:]):
        for n in range(kept.shape[0]):
            tile = kept[n] + got[n]
            for k in range(4):
                out[table[at]] = tile[k * SLICE:(k + 1) * SLICE]
                at += 1


def join(table, *terms):
    return pl.pallas_call(
        join_kernel,
        out_shape=jax.ShapeDtypeStruct((3 * NQ, SLICE, terms[0].shape[2]), jnp.float32),
        in_specs=[SMEM] + [VMEM] * len(terms),
        out_specs=VMEM,
        compiler_params=pltpu.CompilerParams(vmem_limit_bytes=32 * 2**20),
    )(table, *terms)


def walk_perm(dz, flip):
    return [
        (((z + dz) % NZ) * 2 + (x ^ flip), z * 2 + x) for z in range(NZ) for x in range(2)
    ]


def mixed_perm(moves):
    return [
        (source * 2 * NQ + p, target * 2 * NQ + p)
        for p in range(2 * NQ)
        for source, target in walk_perm(*moves[p % 2])
    ]


def solution(mesh):
    tables, pair_perm, single_perm = plan()
    core_swap = [(p, p ^ 1) for p in range(2 * NQ)]
    groups = [[q * 2 + c for q in range(NQ)] for c in range(2)]

    def shards(jacobian, coeffs):
        walk, par = lax.axis_index("walk"), lax.axis_index("par")
        table = lax.dynamic_index_in_dim(
            jnp.asarray(tables), walk * 2 + par % 2, 0, keepdims=False
        )
        tie = lax.optimization_barrier

        def walk_get(value, dz, flip=0):
            return lax.ppermute(value, "walk", walk_perm(dz, flip))

        def mixed_get(value, *moves):
            return lax.ppermute(value, ("walk", "par"), mixed_perm(moves))

        far_a = mixed_get(jacobian, (2, 0), (-3, 0))
        far_b = mixed_get(jacobian, (-3, 0), (2, 0))
        up1 = walk_get(jacobian, 1)
        pair0 = walk_get(jacobian, 0, 1)
        pair1 = walk_get(up1, 0, 1)
        far_a, pair0 = tie((far_a, pair0))
        far_b, pair1 = tie((far_b, pair1))
        late_a = mixed_get(far_a, (1, 0), (0, 1))
        late_b = mixed_get(far_b, (0, 1), (1, 0))
        term = jnp.sum(coeffs[:, None] * jacobian, axis=0)
        near, term = tie((up1, term + walk_get(term, 0, 1)))

        keep, send = products(table, 0, NEARLY, (jacobian, near, far_a, far_b, pair0, pair1), 2**28)
        early = (keep, lax.ppermute(send, "par", core_swap))
        keep, send = products(table, 4 * NEARLY, NLATE, (up1, far_a, far_b, late_a, late_b), 2**35)
        late = (keep, lax.ppermute(send, "par", core_swap))

        mine = join(table, *early, *late).reshape(NQ, 3 * SLICE, -1)
        mine, term = tie((mine, term))
        mine = lax.all_to_all(mine, "par", 0, 0, axis_index_groups=groups, tiled=True)

        after, before = walk_get(term, 4), walk_get(term, -4)
        place = walk // 2 // 4
        first = jnp.where(place == 0, term, jnp.where(place == 1, before, after))
        second = jnp.where(place == 0, after, jnp.where(place == 1, term, before))
        third = jnp.where(place == 0, before, jnp.where(place == 1, after, term))
        term = (first + second) + third
        update = (term + walk_get(term, 2)) + (walk_get(term, 1) + walk_get(term, -1))

        mine = jnp.sum(mine, axis=0)
        pair = lax.ppermute(mine[:2 * SLICE], ("walk", "par"), pair_perm)
        single = lax.ppermute(mine[2 * SLICE:], ("walk", "par"), single_perm)
        gram = jnp.where(
            par % 4 == 1,
            jnp.concatenate((single, pair), axis=0),
            jnp.concatenate((pair, single), axis=0),
        )
        return gram.T, update

    in_specs = (P("walk", "par"), P("walk"))
    out_specs = (P("walk", "par"), P("par"))
    return jax.shard_map(shards, mesh=mesh, in_specs=in_specs, out_specs=out_specs, check_vma=False)
```

```python
import functools

import numpy as np
import jax
import jax.numpy as jnp
from jax import lax
from jax.experimental import pallas as pl
from jax.experimental.pallas import tpu as pltpu
from jax.sharding import PartitionSpec as P

NZ = 12
NQ = 16
SLICE = 32

BLOCKS = ((0, 0), (1, 0), (2, 0), (-3, 0), (0, 1), (1, 1), (3, 0), (-3, 1))
EARLY = (0, 1, 2, 3, 4, 5)
LATE = (1, 2, 3, 6, 7)
NEARLY, NLATE, SHARE = 9, 3, 12

SHARES = (
    (
        ((2, 5), (5, 3), (4, 3), (3, 0), (0, 2), (4, 2), (3, 4), (1, 1), (5, 1), (6, 7), (7, 1), (6, 1)),
        ((2, 3), (1, 3), (0, 3), (3, 2), (2, 4), (2, 1), (0, 1), (4, 1), (3, 1), (3, 6), (7, 2), (2, 7)),
    ),
    (
        ((5, 1), (4, 1), (3, 4), (3, 1), (2, 0), (5, 3), (4, 3), (2, 2), (1, 2), (3, 6), (6, 2), (7, 2)),
        ((2, 4), (3, 0), (2, 3), (1, 3), (0, 3), (2, 5), (0, 2), (4, 2), (3, 2), (6, 7), (7, 1), (2, 7)),
    ),
)


def walker_block(walk, block):
    d, e = BLOCKS[block]
    return 2 * ((walk // 2 + d) % NZ) + (walk % 2 ^ e)


def place_of(index):
    par, slot = divmod(index, 3)
    return (slot + 2) % 3 if par % 4 == 1 else slot


def ring_distance(a, b, n):
    return min((a - b) % n, (b - a) % n)


def distance(source, target):
    (w0, p0), (w1, p1) = source, target
    x0, x1 = (p0 // 16) * 2 + w0 % 2, (p1 // 16) * 2 + w1 % 2
    return (
        ring_distance(w0 // 2, w1 // 2, NZ)
        + ring_distance(x0, x1, 4)
        + ring_distance(p0 // 2 % 8, p1 // 2 % 8, 8)
    )


def assign(walk, core, targets):
    cost = [[distance((walk, q * 2 + core), t) ** 2 for q in range(NQ)] for t in targets]
    pick = []
    for row in cost:
        pick.append(min((q for q in range(NQ) if q not in pick), key=lambda q: row[q]))
    better = True
    while better:
        better = False
        for a in range(NQ):
            for b in range(a):
                now = cost[a][pick[a]] + cost[b][pick[b]]
                if cost[a][pick[b]] + cost[b][pick[a]] < now:
                    pick[a], pick[b] = pick[b], pick[a]
                    better = True
    return pick


def held(block, core):
    return block ^ 1 if core and block in (2, 3, 6, 7) else block


def plan():
    early_table = np.zeros((2 * NZ, 2, 2, NEARLY, 2), np.int32)
    late_table = np.zeros((2 * NZ, 2, 2, NLATE, 2), np.int32)
    places = np.zeros((2 * NZ, 2, SHARE, 4), np.int32)
    pairs = [[], [], []]
    seen = set()
    for walk in range(2 * NZ):
        for core, share in enumerate(SHARES[walk % 2]):
            slices = []
            for n, (row, col) in enumerate(share):
                for k in range(4):
                    index = 4 * walker_block(walk, col) + k
                    target = (walker_block(walk, row), index // 3)
                    slices.append((n, k, place_of(index), target))
            for slot in range(3):
                chosen = [s for s in slices if s[2] == slot]
                if slot != 1:
                    picks = assign(walk, core, [s[3] for s in chosen])
                for (n, k, _, target), q in zip(chosen, picks, strict=True):
                    places[walk, core, n, k] = q * 3 + slot
                    source = walk * 2 * NQ + q * 2 + core
                    pairs[slot].append((source, target[0] * 2 * NQ + target[1]))
                    seen.add((target, slot))
            for n, (row, col) in enumerate(share):
                for mine in range(2):
                    at = [held(row, mine), held(col, mine)]
                    if n < NEARLY:
                        early_table[walk, mine, int(core != mine), n] = [EARLY.index(b) for b in at]
                    else:
                        late_table[walk, mine, int(core != mine), n - NEARLY] = [LATE.index(b) for b in at]
    assert len(seen) == NZ * 2 * 2 * NQ * 3
    assert sorted(pairs[0]) == sorted(pairs[1])
    tables = [t.reshape(4 * NZ, -1) for t in (early_table, late_table, places)]
    return np.concatenate(tables, axis=1), pairs[0], pairs[2]


def product_kernel(base, count, table, *refs):
    *blocks, keep, send, parts = refs
    depth = blocks[0].shape[1]
    for b, ref in enumerate(blocks):
        value = ref[...]
        high = value.astype(jnp.bfloat16)
        parts[b, :, :depth] = high
        parts[b, :, depth:] = (value - high.astype(jnp.float32)).astype(jnp.bfloat16)
    dims = (((1,), (1,)), ((), ()))

    def dot(left, right):
        return lax.dot_general(left, right, dims, preferred_element_type=jnp.float32)

    for half, out in ((1, send), (0, keep)):
        for n in range(count):
            at = base + (half * count + n) * 2
            row, col = table[at], table[at + 1]
            row_high, row_low = parts[row, :, :depth], parts[row, :, depth:]
            col_high, col_low = parts[col, :, :depth], parts[col, :, depth:]
            out[n] = dot(col_high, row_high) + (dot(col_high, row_low) + dot(col_low, row_high))


VMEM = pl.BlockSpec(memory_space=pltpu.VMEM)
SMEM = pl.BlockSpec(memory_space=pltpu.SMEM)


def products(table, base, count, blocks, cost):
    rows, depth = blocks[0].shape
    out = jax.ShapeDtypeStruct((count, rows, rows), jnp.float32)
    return pl.pallas_call(
        functools.partial(product_kernel, base, count),
        out_shape=(out, out),
        in_specs=[SMEM] + [VMEM] * len(blocks),
        out_specs=(VMEM, VMEM),
        scratch_shapes=[pltpu.VMEM((len(blocks), rows, 2 * depth), jnp.bfloat16)],
        compiler_params=pltpu.CompilerParams(vmem_limit_bytes=32 * 2**20),
        cost_estimate=pl.CostEstimate(flops=cost, bytes_accessed=2**20, transcendentals=0),
    )(table, *blocks)


def join_kernel(table, *refs):
    *terms, out = refs
    at = 4 * SHARE
    for kept, got in (terms[:2], terms[2:]):
        for n in range(kept.shape[0]):
            tile = kept[n] + got[n]
            for k in range(4):
                out[table[at]] = tile[k * SLICE:(k + 1) * SLICE]
                at += 1


def join(table, *terms):
    return pl.pallas_call(
        join_kernel,
        out_shape=jax.ShapeDtypeStruct((3 * NQ, SLICE, terms[0].shape[2]), jnp.float32),
        in_specs=[SMEM] + [VMEM] * len(terms),
        out_specs=VMEM,
        compiler_params=pltpu.CompilerParams(vmem_limit_bytes=32 * 2**20),
    )(table, *terms)


def walk_perm(dz, flip):
    return [
        (((z + dz) % NZ) * 2 + (x ^ flip), z * 2 + x) for z in range(NZ) for x in range(2)
    ]


def mixed_perm(moves):
    return [
        (source * 2 * NQ + p, target * 2 * NQ + p)
        for p in range(2 * NQ)
        for source, target in walk_perm(*moves[p % 2])
    ]


def solution(mesh):
    tables, pair_perm, single_perm = plan()
    core_swap = [(p, p ^ 1) for p in range(2 * NQ)]
    groups = [[q * 2 + c for q in range(NQ)] for c in range(2)]

    def shards(jacobian, coeffs):
        walk, par = lax.axis_index("walk"), lax.axis_index("par")
        table = lax.dynamic_index_in_dim(
            jnp.asarray(tables), walk * 2 + par % 2, 0, keepdims=False
        )
        tie = lax.optimization_barrier

        def walk_get(value, dz, flip=0):
            return lax.ppermute(value, "walk", walk_perm(dz, flip))

        def mixed_get(value, *moves):
            return lax.ppermute(value, ("walk", "par"), mixed_perm(moves))

        far_a = mixed_get(jacobian, (2, 0), (-3, 0))
        far_b = mixed_get(jacobian, (-3, 0), (2, 0))
        up1 = walk_get(jacobian, 1)
        pair0 = walk_get(jacobian, 0, 1)
        pair1 = walk_get(up1, 0, 1)
        term = jnp.sum(coeffs[:, None] * jacobian, axis=0)
        far_a, pair0, term = tie((far_a, pair0, term + walk_get(term, 0, 1)))
        far_b, pair1 = tie((far_b, pair1))
        late_a = mixed_get(far_a, (1, 0), (0, 1))
        late_b = mixed_get(far_b, (0, 1), (1, 0))

        keep, send = products(table, 0, NEARLY, (jacobian, up1, far_a, far_b, pair0, pair1), 2**28)
        early = (keep, lax.ppermute(send, "par", core_swap))
        keep, send = products(table, 4 * NEARLY, NLATE, (up1, far_a, far_b, late_a, late_b), 2**35)
        late = (keep, lax.ppermute(send, "par", core_swap))

        mine = join(table, *early, *late).reshape(NQ, 3 * SLICE, -1)
        mine, term = tie((mine, term))
        mine = lax.all_to_all(mine, "par", 0, 0, axis_index_groups=groups, tiled=True)

        after, before = walk_get(term, 4), walk_get(term, -4)
        place = walk // 2 // 4
        first = jnp.where(place == 0, term, jnp.where(place == 1, before, after))
        second = jnp.where(place == 0, after, jnp.where(place == 1, term, before))
        third = jnp.where(place == 0, before, jnp.where(place == 1, after, term))
        term = (first + second) + third
        update = (term + walk_get(term, 2)) + (walk_get(term, 1) + walk_get(term, -1))

        mine = jnp.sum(mine, axis=0)
        pair = lax.ppermute(mine[:2 * SLICE], ("walk", "par"), pair_perm)
        single = lax.ppermute(mine[2 * SLICE:], ("walk", "par"), single_perm)
        gram = jnp.where(
            par % 4 == 1,
            jnp.concatenate((single, pair), axis=0),
            jnp.concatenate((pair, single), axis=0),
        )
        return gram.T, update

    in_specs = (P("walk", "par"), P("walk"))
    out_specs = (P("walk", "par"), P("par"))
    return jax.shard_map(shards, mesh=mesh, in_specs=in_specs, out_specs=out_specs, check_vma=False)
```

```python
import functools

import numpy as np
import jax
import jax.numpy as jnp
from jax import lax
from jax.experimental import pallas as pl
from jax.experimental.pallas import tpu as pltpu
from jax.sharding import PartitionSpec as P

NZ = 12
NQ = 16
SLICE = 32

BLOCKS = ((0, 0), (1, 0), (2, 0), (-3, 0), (0, 1), (1, 1), (3, 0), (-3, 1))
EARLY = (0, 1, 2, 3, 4, 5)
LATE = (1, 2, 3, 6, 7)
NEARLY, NLATE, SHARE = 9, 3, 12

SHARES = (
    (
        ((2, 5), (5, 3), (4, 3), (3, 0), (0, 2), (4, 2), (3, 4), (1, 1), (5, 1), (6, 7), (7, 1), (6, 1)),
        ((2, 3), (1, 3), (0, 3), (3, 2), (2, 4), (2, 1), (0, 1), (4, 1), (3, 1), (3, 6), (7, 2), (2, 7)),
    ),
    (
        ((5, 1), (4, 1), (3, 4), (3, 1), (2, 0), (5, 3), (4, 3), (2, 2), (1, 2), (3, 6), (6, 2), (7, 2)),
        ((2, 4), (3, 0), (2, 3), (1, 3), (0, 3), (2, 5), (0, 2), (4, 2), (3, 2), (6, 7), (7, 1), (2, 7)),
    ),
)


def walker_block(walk, block):
    d, e = BLOCKS[block]
    return 2 * ((walk // 2 + d) % NZ) + (walk % 2 ^ e)


def place_of(index):
    par, slot = divmod(index, 3)
    return (slot + 2) % 3 if par % 4 == 1 else slot


def ring_distance(a, b, n):
    return min((a - b) % n, (b - a) % n)


def distance(source, target):
    (w0, p0), (w1, p1) = source, target
    x0, x1 = (p0 // 16) * 2 + w0 % 2, (p1 // 16) * 2 + w1 % 2
    return (
        ring_distance(w0 // 2, w1 // 2, NZ)
        + ring_distance(x0, x1, 4)
        + ring_distance(p0 // 2 % 8, p1 // 2 % 8, 8)
    )


def assign(walk, core, targets):
    cost = [[distance((walk, q * 2 + core), t) ** 2 for q in range(NQ)] for t in targets]
    pick = []
    for row in cost:
        pick.append(min((q for q in range(NQ) if q not in pick), key=lambda q: row[q]))
    better = True
    while better:
        better = False
        for a in range(NQ):
            for b in range(a):
                now = cost[a][pick[a]] + cost[b][pick[b]]
                if cost[a][pick[b]] + cost[b][pick[a]] < now:
                    pick[a], pick[b] = pick[b], pick[a]
                    better = True
    return pick


def held(block, core):
    return block ^ 1 if core and block in (2, 3, 6, 7) else block


def plan():
    early_table = np.zeros((2 * NZ, 2, 2, NEARLY, 2), np.int32)
    late_table = np.zeros((2 * NZ, 2, 2, NLATE, 2), np.int32)
    places = np.zeros((2 * NZ, 2, SHARE, 4), np.int32)
    pairs = [[], [], []]
    seen = set()
    for walk in range(2 * NZ):
        for core, share in enumerate(SHARES[walk % 2]):
            slices = []
            for n, (row, col) in enumerate(share):
                for k in range(4):
                    index = 4 * walker_block(walk, col) + k
                    target = (walker_block(walk, row), index // 3)
                    slices.append((n, k, place_of(index), target))
            for slot in range(3):
                chosen = [s for s in slices if s[2] == slot]
                if slot != 1:
                    picks = assign(walk, core, [s[3] for s in chosen])
                for (n, k, _, target), q in zip(chosen, picks, strict=True):
                    places[walk, core, n, k] = q * 3 + slot
                    source = walk * 2 * NQ + q * 2 + core
                    pairs[slot].append((source, target[0] * 2 * NQ + target[1]))
                    seen.add((target, slot))
            for n, (row, col) in enumerate(share):
                for mine in range(2):
                    at = [held(row, mine), held(col, mine)]
                    if n < NEARLY:
                        early_table[walk, mine, int(core != mine), n] = [EARLY.index(b) for b in at]
                    else:
                        late_table[walk, mine, int(core != mine), n - NEARLY] = [LATE.index(b) for b in at]
    assert len(seen) == NZ * 2 * 2 * NQ * 3
    assert sorted(pairs[0]) == sorted(pairs[1])
    tables = [t.reshape(4 * NZ, -1) for t in (early_table, late_table, places)]
    return np.concatenate(tables, axis=1), pairs[0], pairs[2]


def product_kernel(base, count, table, *refs):
    *blocks, keep, send, parts = refs
    depth = blocks[0].shape[1]
    for b, ref in enumerate(blocks):
        value = ref[...]
        high = value.astype(jnp.bfloat16)
        parts[b, :, :depth] = high
        parts[b, :, depth:] = (value - high.astype(jnp.float32)).astype(jnp.bfloat16)
    dims = (((1,), (1,)), ((), ()))

    def dot(left, right):
        return lax.dot_general(left, right, dims, preferred_element_type=jnp.float32)

    for half, out in ((1, send), (0, keep)):
        for n in range(count):
            at = base + (half * count + n) * 2
            row, col = table[at], table[at + 1]
            row_high, row_low = parts[row, :, :depth], parts[row, :, depth:]
            col_high, col_low = parts[col, :, :depth], parts[col, :, depth:]
            out[n] = dot(col_high, row_high) + (dot(col_high, row_low) + dot(col_low, row_high))


VMEM = pl.BlockSpec(memory_space=pltpu.VMEM)
SMEM = pl.BlockSpec(memory_space=pltpu.SMEM)


def products(table, base, count, blocks, cost):
    rows, depth = blocks[0].shape
    out = jax.ShapeDtypeStruct((count, rows, rows), jnp.float32)
    return pl.pallas_call(
        functools.partial(product_kernel, base, count),
        out_shape=(out, out),
        in_specs=[SMEM] + [VMEM] * len(blocks),
        out_specs=(VMEM, VMEM),
        scratch_shapes=[pltpu.VMEM((len(blocks), rows, 2 * depth), jnp.bfloat16)],
        compiler_params=pltpu.CompilerParams(vmem_limit_bytes=32 * 2**20),
        cost_estimate=pl.CostEstimate(flops=cost, bytes_accessed=2**20, transcendentals=0),
    )(table, *blocks)


def join_kernel(table, *refs):
    *terms, out = refs
    at = 4 * SHARE
    for kept, got in (terms[:2], terms[2:]):
        for n in range(kept.shape[0]):
            tile = kept[n] + got[n]
            for k in range(4):
                out[table[at]] = tile[k * SLICE:(k + 1) * SLICE]
                at += 1


def join(table, *terms):
    return pl.pallas_call(
        join_kernel,
        out_shape=jax.ShapeDtypeStruct((3 * NQ, SLICE, terms[0].shape[2]), jnp.float32),
        in_specs=[SMEM] + [VMEM] * len(terms),
        out_specs=VMEM,
        compiler_params=pltpu.CompilerParams(vmem_limit_bytes=32 * 2**20),
    )(table, *terms)


def walk_perm(dz, flip):
    return [
        (((z + dz) % NZ) * 2 + (x ^ flip), z * 2 + x) for z in range(NZ) for x in range(2)
    ]


def mixed_perm(moves):
    return [
        (source * 2 * NQ + p, target * 2 * NQ + p)
        for p in range(2 * NQ)
        for source, target in walk_perm(*moves[p % 2])
    ]


def solution(mesh):
    tables, pair_perm, single_perm = plan()
    core_swap = [(p, p ^ 1) for p in range(2 * NQ)]
    groups = [[q * 2 + c for q in range(NQ)] for c in range(2)]

    def shards(jacobian, coeffs):
        walk, par = lax.axis_index("walk"), lax.axis_index("par")
        table = lax.dynamic_index_in_dim(
            jnp.asarray(tables), walk * 2 + par % 2, 0, keepdims=False
        )
        tie = lax.optimization_barrier

        def walk_get(value, dz, flip=0):
            return lax.ppermute(value, "walk", walk_perm(dz, flip))

        def mixed_get(value, *moves):
            return lax.ppermute(value, ("walk", "par"), mixed_perm(moves))

        far_a = mixed_get(jacobian, (2, 0), (-3, 0))
        far_b = mixed_get(jacobian, (-3, 0), (2, 0))
        up1 = walk_get(jacobian, 1)
        pair0 = walk_get(jacobian, 0, 1)
        pair1 = walk_get(up1, 0, 1)
        term = jnp.sum(coeffs[:, None] * jacobian, axis=0)
        far_a, term = tie((far_a, term + walk_get(term, 0, 1)))
        far_b, pair1 = tie((far_b, pair1))
        late_a = mixed_get(far_a, (1, 0), (0, 1))
        late_b = mixed_get(far_b, (0, 1), (1, 0))

        keep, send = products(table, 0, NEARLY, (jacobian, up1, far_a, far_b, pair0, pair1), 2**28)
        early = (keep, lax.ppermute(send, "par", core_swap))
        keep, send = products(table, 4 * NEARLY, NLATE, (up1, far_a, far_b, late_a, late_b), 2**35)
        late = (keep, lax.ppermute(send, "par", core_swap))

        mine = join(table, *early, *late).reshape(NQ, 3 * SLICE, -1)
        mine, term = tie((mine, term))
        mine = lax.all_to_all(mine, "par", 0, 0, axis_index_groups=groups, tiled=True)

        after, before = walk_get(term, 4), walk_get(term, -4)
        place = walk // 2 // 4
        first = jnp.where(place == 0, term, jnp.where(place == 1, before, after))
        second = jnp.where(place == 0, after, jnp.where(place == 1, term, before))
        third = jnp.where(place == 0, before, jnp.where(place == 1, after, term))
        term = (first + second) + third
        update = (term + walk_get(term, 2)) + (walk_get(term, 1) + walk_get(term, -1))

        mine = jnp.sum(mine, axis=0)
        pair = lax.ppermute(mine[:2 * SLICE], ("walk", "par"), pair_perm)
        single = lax.ppermute(mine[2 * SLICE:], ("walk", "par"), single_perm)
        gram = jnp.where(
            par % 4 == 1,
            jnp.concatenate((single, pair), axis=0),
            jnp.concatenate((pair, single), axis=0),
        )
        return gram.T, update

    in_specs = (P("walk", "par"), P("walk"))
    out_specs = (P("walk", "par"), P("par"))
    return jax.shard_map(shards, mesh=mesh, in_specs=in_specs, out_specs=out_specs, check_vma=False)
```

```python
import functools

import numpy as np
import jax
import jax.numpy as jnp
from jax import lax
from jax.experimental import pallas as pl
from jax.experimental.pallas import tpu as pltpu
from jax.sharding import PartitionSpec as P

NZ = 12
NQ = 16
SLICE = 32

BLOCKS = ((0, 0), (1, 0), (2, 0), (-3, 0), (0, 1), (1, 1), (3, 0), (-3, 1))
EARLY = (0, 1, 2, 3, 4, 5)
LATE = (1, 2, 3, 6, 7)
NEARLY, NLATE, SHARE = 9, 3, 12

SHARES = (
    (
        ((2, 5), (5, 3), (4, 3), (3, 0), (0, 2), (4, 2), (3, 4), (1, 1), (5, 1), (6, 7), (7, 1), (6, 1)),
        ((2, 3), (1, 3), (0, 3), (3, 2), (2, 4), (2, 1), (0, 1), (4, 1), (3, 1), (3, 6), (7, 2), (2, 7)),
    ),
    (
        ((5, 1), (4, 1), (3, 4), (3, 1), (2, 0), (5, 3), (4, 3), (2, 2), (1, 2), (3, 6), (6, 2), (7, 2)),
        ((2, 4), (3, 0), (2, 3), (1, 3), (0, 3), (2, 5), (0, 2), (4, 2), (3, 2), (6, 7), (7, 1), (2, 7)),
    ),
)


def walker_block(walk, block):
    d, e = BLOCKS[block]
    return 2 * ((walk // 2 + d) % NZ) + (walk % 2 ^ e)


def place_of(index):
    par, slot = divmod(index, 3)
    return (slot + 2) % 3 if par % 4 == 1 else slot


def ring_distance(a, b, n):
    return min((a - b) % n, (b - a) % n)


def distance(source, target):
    (w0, p0), (w1, p1) = source, target
    x0, x1 = (p0 // 16) * 2 + w0 % 2, (p1 // 16) * 2 + w1 % 2
    return (
        ring_distance(w0 // 2, w1 // 2, NZ)
        + ring_distance(x0, x1, 4)
        + ring_distance(p0 // 2 % 8, p1 // 2 % 8, 8)
    )


def assign(walk, core, targets):
    cost = [[distance((walk, q * 2 + core), t) ** 2 for q in range(NQ)] for t in targets]
    pick = []
    for row in cost:
        pick.append(min((q for q in range(NQ) if q not in pick), key=lambda q: row[q]))
    better = True
    while better:
        better = False
        for a in range(NQ):
            for b in range(a):
                now = cost[a][pick[a]] + cost[b][pick[b]]
                if cost[a][pick[b]] + cost[b][pick[a]] < now:
                    pick[a], pick[b] = pick[b], pick[a]
                    better = True
    return pick


def held(block, core):
    return block ^ 1 if core and block in (2, 3, 6, 7) else block


def plan():
    early_table = np.zeros((2 * NZ, 2, 2, NEARLY, 2), np.int32)
    late_table = np.zeros((2 * NZ, 2, 2, NLATE, 2), np.int32)
    places = np.zeros((2 * NZ, 2, SHARE, 4), np.int32)
    pairs = [[], [], []]
    seen = set()
    for walk in range(2 * NZ):
        for core, share in enumerate(SHARES[walk % 2]):
            slices = []
            for n, (row, col) in enumerate(share):
                for k in range(4):
                    index = 4 * walker_block(walk, col) + k
                    target = (walker_block(walk, row), index // 3)
                    slices.append((n, k, place_of(index), target))
            for slot in range(3):
                chosen = [s for s in slices if s[2] == slot]
                if slot != 1:
                    picks = assign(walk, core, [s[3] for s in chosen])
                for (n, k, _, target), q in zip(chosen, picks, strict=True):
                    places[walk, core, n, k] = q * 3 + slot
                    source = walk * 2 * NQ + q * 2 + core
                    pairs[slot].append((source, target[0] * 2 * NQ + target[1]))
                    seen.add((target, slot))
            for n, (row, col) in enumerate(share):
                for mine in range(2):
                    at = [held(row, mine), held(col, mine)]
                    if n < NEARLY:
                        early_table[walk, mine, int(core != mine), n] = [EARLY.index(b) for b in at]
                    else:
                        late_table[walk, mine, int(core != mine), n - NEARLY] = [LATE.index(b) for b in at]
    assert len(seen) == NZ * 2 * 2 * NQ * 3
    assert sorted(pairs[0]) == sorted(pairs[1])
    tables = [t.reshape(4 * NZ, -1) for t in (early_table, late_table, places)]
    return np.concatenate(tables, axis=1), pairs[0], pairs[2]


def product_kernel(base, count, table, *refs):
    *blocks, keep, send, parts = refs
    depth = blocks[0].shape[1]
    for b, ref in enumerate(blocks):
        value = ref[...]
        high = value.astype(jnp.bfloat16)
        parts[b, :, :depth] = high
        parts[b, :, depth:] = (value - high.astype(jnp.float32)).astype(jnp.bfloat16)
    dims = (((1,), (1,)), ((), ()))

    def dot(left, right):
        return lax.dot_general(left, right, dims, preferred_element_type=jnp.float32)

    for half, out in ((1, send), (0, keep)):
        for n in range(count):
            at = base + (half * count + n) * 2
            row, col = table[at], table[at + 1]
            row_high, row_low = parts[row, :, :depth], parts[row, :, depth:]
            col_high, col_low = parts[col, :, :depth], parts[col, :, depth:]
            out[n] = dot(col_high, row_high) + (dot(col_high, row_low) + dot(col_low, row_high))


VMEM = pl.BlockSpec(memory_space=pltpu.VMEM)
SMEM = pl.BlockSpec(memory_space=pltpu.SMEM)


def products(table, base, count, blocks, cost):
    rows, depth = blocks[0].shape
    out = jax.ShapeDtypeStruct((count, rows, rows), jnp.float32)
    return pl.pallas_call(
        functools.partial(product_kernel, base, count),
        out_shape=(out, out),
        in_specs=[SMEM] + [VMEM] * len(blocks),
        out_specs=(VMEM, VMEM),
        scratch_shapes=[pltpu.VMEM((len(blocks), rows, 2 * depth), jnp.bfloat16)],
        compiler_params=pltpu.CompilerParams(vmem_limit_bytes=32 * 2**20),
        cost_estimate=pl.CostEstimate(flops=cost, bytes_accessed=2**20, transcendentals=0),
    )(table, *blocks)


def join_kernel(table, *refs):
    *terms, out = refs
    at = 4 * SHARE
    for kept, got in (terms[:2], terms[2:]):
        for n in range(kept.shape[0]):
            tile = kept[n] + got[n]
            for k in range(4):
                out[table[at]] = tile[k * SLICE:(k + 1) * SLICE]
                at += 1


def join(table, *terms):
    return pl.pallas_call(
        join_kernel,
        out_shape=jax.ShapeDtypeStruct((3 * NQ, SLICE, terms[0].shape[2]), jnp.float32),
        in_specs=[SMEM] + [VMEM] * len(terms),
        out_specs=VMEM,
        compiler_params=pltpu.CompilerParams(vmem_limit_bytes=32 * 2**20),
    )(table, *terms)


def walk_perm(dz, flip):
    return [
        (((z + dz) % NZ) * 2 + (x ^ flip), z * 2 + x) for z in range(NZ) for x in range(2)
    ]


def mixed_perm(moves):
    return [
        (source * 2 * NQ + p, target * 2 * NQ + p)
        for p in range(2 * NQ)
        for source, target in walk_perm(*moves[p % 2])
    ]


def solution(mesh):
    tables, pair_perm, single_perm = plan()
    core_swap = [(p, p ^ 1) for p in range(2 * NQ)]
    groups = [[q * 2 + c for q in range(NQ)] for c in range(2)]

    def shards(jacobian, coeffs):
        walk, par = lax.axis_index("walk"), lax.axis_index("par")
        table = lax.dynamic_index_in_dim(
            jnp.asarray(tables), walk * 2 + par % 2, 0, keepdims=False
        )
        tie = lax.optimization_barrier

        def walk_get(value, dz, flip=0):
            return lax.ppermute(value, "walk", walk_perm(dz, flip))

        def mixed_get(value, *moves):
            return lax.ppermute(value, ("walk", "par"), mixed_perm(moves))

        far_a = mixed_get(jacobian, (2, 0), (-3, 0))
        far_b = mixed_get(jacobian, (-3, 0), (2, 0))
        up1 = walk_get(jacobian, 1)
        pair0 = walk_get(jacobian, 0, 1)
        pair1 = walk_get(up1, 0, 1)
        term = jnp.sum(coeffs[:, None] * jacobian, axis=0)
        far_a, pair0, term, table = tie((far_a, pair0, term + walk_get(term, 0, 1), table))
        far_b, pair1 = tie((far_b, pair1))
        late_a = mixed_get(far_a, (1, 0), (0, 1))
        late_b = mixed_get(far_b, (0, 1), (1, 0))

        keep, send = products(table, 0, NEARLY, (jacobian, up1, far_a, far_b, pair0, pair1), 2**28)
        early = (keep, lax.ppermute(send, "par", core_swap))
        keep, send = products(table, 4 * NEARLY, NLATE, (up1, far_a, far_b, late_a, late_b), 2**35)
        late = (keep, lax.ppermute(send, "par", core_swap))

        mine = join(table, *early, *late).reshape(NQ, 3 * SLICE, -1)
        mine, term = tie((mine, term))
        mine = lax.all_to_all(mine, "par", 0, 0, axis_index_groups=groups, tiled=True)

        after, before = walk_get(term, 4), walk_get(term, -4)
        place = walk // 2 // 4
        first = jnp.where(place == 0, term, jnp.where(place == 1, before, after))
        second = jnp.where(place == 0, after, jnp.where(place == 1, term, before))
        third = jnp.where(place == 0, before, jnp.where(place == 1, after, term))
        term = (first + second) + third
        update = (term + walk_get(term, 2)) + (walk_get(term, 1) + walk_get(term, -1))

        mine = jnp.sum(mine, axis=0)
        pair = lax.ppermute(mine[:2 * SLICE], ("walk", "par"), pair_perm)
        single = lax.ppermute(mine[2 * SLICE:], ("walk", "par"), single_perm)
        gram = jnp.where(
            par % 4 == 1,
            jnp.concatenate((single, pair), axis=0),
            jnp.concatenate((pair, single), axis=0),
        )
        return gram.T, update

    in_specs = (P("walk", "par"), P("walk"))
    out_specs = (P("walk", "par"), P("par"))
    return jax.shard_map(shards, mesh=mesh, in_specs=in_specs, out_specs=out_specs, check_vma=False)
```

```python
import functools

import numpy as np
import jax
import jax.numpy as jnp
from jax import lax
from jax.experimental import pallas as pl
from jax.experimental.pallas import tpu as pltpu
from jax.sharding import PartitionSpec as P

NZ = 12
NQ = 16
SLICE = 32

BLOCKS = ((0, 0), (1, 0), (2, 0), (-3, 0), (0, 1), (1, 1), (3, 0), (-3, 1))
EARLY = (0, 1, 2, 3, 4, 5)
LATE = (1, 2, 3, 6, 7)
NEARLY, NLATE, SHARE = 9, 3, 12

SHARES = (
    (
        ((2, 5), (5, 3), (4, 3), (3, 0), (0, 2), (4, 2), (3, 4), (1, 1), (5, 1), (6, 7), (7, 1), (6, 1)),
        ((2, 3), (1, 3), (0, 3), (3, 2), (2, 4), (2, 1), (0, 1), (4, 1), (3, 1), (3, 6), (7, 2), (2, 7)),
    ),
    (
        ((5, 1), (4, 1), (3, 4), (3, 1), (2, 0), (5, 3), (4, 3), (2, 2), (1, 2), (3, 6), (6, 2), (7, 2)),
        ((2, 4), (3, 0), (2, 3), (1, 3), (0, 3), (2, 5), (0, 2), (4, 2), (3, 2), (6, 7), (7, 1), (2, 7)),
    ),
)


def walker_block(walk, block):
    d, e = BLOCKS[block]
    return 2 * ((walk // 2 + d) % NZ) + (walk % 2 ^ e)


def place_of(index):
    par, slot = divmod(index, 3)
    return (slot + 2) % 3 if par % 4 == 1 else slot


def ring_distance(a, b, n):
    return min((a - b) % n, (b - a) % n)


def distance(source, target):
    (w0, p0), (w1, p1) = source, target
    x0, x1 = (p0 // 16) * 2 + w0 % 2, (p1 // 16) * 2 + w1 % 2
    return (
        ring_distance(w0 // 2, w1 // 2, NZ)
        + ring_distance(x0, x1, 4)
        + ring_distance(p0 // 2 % 8, p1 // 2 % 8, 8)
    )


def assign(walk, core, targets):
    cost = [[distance((walk, q * 2 + core), t) ** 2 for q in range(NQ)] for t in targets]
    pick = []
    for row in cost:
        pick.append(min((q for q in range(NQ) if q not in pick), key=lambda q: row[q]))
    better = True
    while better:
        better = False
        for a in range(NQ):
            for b in range(a):
                now = cost[a][pick[a]] + cost[b][pick[b]]
                if cost[a][pick[b]] + cost[b][pick[a]] < now:
                    pick[a], pick[b] = pick[b], pick[a]
                    better = True
    return pick


def held(block, core):
    return block ^ 1 if core and block in (2, 3, 6, 7) else block


def plan():
    early_table = np.zeros((2 * NZ, 2, 2, NEARLY, 2), np.int32)
    late_table = np.zeros((2 * NZ, 2, 2, NLATE, 2), np.int32)
    places = np.zeros((2 * NZ, 2, SHARE, 4), np.int32)
    pairs = [[], [], []]
    seen = set()
    for walk in range(2 * NZ):
        for core, share in enumerate(SHARES[walk % 2]):
            slices = []
            for n, (row, col) in enumerate(share):
                for k in range(4):
                    index = 4 * walker_block(walk, col) + k
                    target = (walker_block(walk, row), index // 3)
                    slices.append((n, k, place_of(index), target))
            for slot in range(3):
                chosen = [s for s in slices if s[2] == slot]
                if slot != 1:
                    picks = assign(walk, core, [s[3] for s in chosen])
                for (n, k, _, target), q in zip(chosen, picks, strict=True):
                    places[walk, core, n, k] = q * 3 + slot
                    source = walk * 2 * NQ + q * 2 + core
                    pairs[slot].append((source, target[0] * 2 * NQ + target[1]))
                    seen.add((target, slot))
            for n, (row, col) in enumerate(share):
                for mine in range(2):
                    at = [held(row, mine), held(col, mine)]
                    if n < NEARLY:
                        early_table[walk, mine, int(core != mine), n] = [EARLY.index(b) for b in at]
                    else:
                        late_table[walk, mine, int(core != mine), n - NEARLY] = [LATE.index(b) for b in at]
    assert len(seen) == NZ * 2 * 2 * NQ * 3
    assert sorted(pairs[0]) == sorted(pairs[1])
    tables = [t.reshape(4 * NZ, -1) for t in (early_table, late_table, places)]
    return np.concatenate(tables, axis=1), pairs[0], pairs[2]


def product_kernel(base, count, table, *refs):
    *blocks, keep, send, parts = refs
    depth = blocks[0].shape[1]
    for b, ref in enumerate(blocks):
        value = ref[...]
        high = value.astype(jnp.bfloat16)
        parts[b, :, :depth] = high
        parts[b, :, depth:] = (value - high.astype(jnp.float32)).astype(jnp.bfloat16)
    dims = (((1,), (1,)), ((), ()))

    def dot(left, right):
        return lax.dot_general(left, right, dims, preferred_element_type=jnp.float32)

    for half, out in ((1, send), (0, keep)):
        for n in range(count):
            at = base + (half * count + n) * 2
            row, col = table[at], table[at + 1]
            row_high, row_low = parts[row, :, :depth], parts[row, :, depth:]
            col_high, col_low = parts[col, :, :depth], parts[col, :, depth:]
            out[n] = dot(col_high, row_high) + (dot(col_high, row_low) + dot(col_low, row_high))


VMEM = pl.BlockSpec(memory_space=pltpu.VMEM)
SMEM = pl.BlockSpec(memory_space=pltpu.SMEM)


def products(table, base, count, blocks, cost):
    rows, depth = blocks[0].shape
    out = jax.ShapeDtypeStruct((count, rows, rows), jnp.float32)
    return pl.pallas_call(
        functools.partial(product_kernel, base, count),
        out_shape=(out, out),
        in_specs=[SMEM] + [VMEM] * len(blocks),
        out_specs=(VMEM, VMEM),
        scratch_shapes=[pltpu.VMEM((len(blocks), rows, 2 * depth), jnp.bfloat16)],
        compiler_params=pltpu.CompilerParams(vmem_limit_bytes=32 * 2**20),
        cost_estimate=pl.CostEstimate(flops=cost, bytes_accessed=2**20, transcendentals=0),
    )(table, *blocks)


def join_kernel(table, *refs):
    *terms, out = refs
    at = 4 * SHARE
    for kept, got in (terms[:2], terms[2:]):
        for n in range(kept.shape[0]):
            tile = kept[n] + got[n]
            for k in range(4):
                out[table[at]] = tile[k * SLICE:(k + 1) * SLICE]
                at += 1


def join(table, *terms):
    return pl.pallas_call(
        join_kernel,
        out_shape=jax.ShapeDtypeStruct((3 * NQ, SLICE, terms[0].shape[2]), jnp.float32),
        in_specs=[SMEM] + [VMEM] * len(terms),
        out_specs=VMEM,
        compiler_params=pltpu.CompilerParams(vmem_limit_bytes=32 * 2**20),
    )(table, *terms)


def walk_perm(dz, flip):
    return [
        (((z + dz) % NZ) * 2 + (x ^ flip), z * 2 + x) for z in range(NZ) for x in range(2)
    ]


def mixed_perm(moves):
    return [
        (source * 2 * NQ + p, target * 2 * NQ + p)
        for p in range(2 * NQ)
        for source, target in walk_perm(*moves[p % 2])
    ]


def solution(mesh):
    tables, pair_perm, single_perm = plan()
    core_swap = [(p, p ^ 1) for p in range(2 * NQ)]
    groups = [[q * 2 + c for q in range(NQ)] for c in range(2)]

    def shards(jacobian, coeffs):
        walk, par = lax.axis_index("walk"), lax.axis_index("par")
        table = lax.dynamic_index_in_dim(
            jnp.asarray(tables), walk * 2 + par % 2, 0, keepdims=False
        )
        tie = lax.optimization_barrier

        def walk_get(value, dz, flip=0):
            return lax.ppermute(value, "walk", walk_perm(dz, flip))

        def mixed_get(value, *moves):
            return lax.ppermute(value, ("walk", "par"), mixed_perm(moves))

        far_a = mixed_get(jacobian, (2, 0), (-3, 0))
        far_b = mixed_get(jacobian, (-3, 0), (2, 0))
        up1 = walk_get(jacobian, 1)
        pair0 = walk_get(jacobian, 0, 1)
        pair1 = walk_get(up1, 0, 1)
        term = jnp.sum(coeffs[:, None] * jacobian, axis=0)
        far_a, pair0, term, table = tie((far_a, pair0, term + walk_get(term, 0, 1), table))
        far_b, pair1 = tie((far_b, pair1))
        late_a = mixed_get(far_a, (1, 0), (0, 1))
        late_b = mixed_get(far_b, (0, 1), (1, 0))

        keep, send = products(table, 0, NEARLY, (jacobian, up1, far_a, far_b, pair0, pair1), 2**28)
        early = (keep, lax.ppermute(send, "par", core_swap))
        keep, send = products(table, 4 * NEARLY, NLATE, (up1, far_a, far_b, late_a, late_b), 2**35)
        late = (keep, lax.ppermute(send, "par", core_swap))

        mine = join(table, *early, *late).reshape(NQ, 3 * SLICE, -1)
        mine, term = tie((mine, term))
        mine = lax.all_to_all(mine, "par", 0, 0, axis_index_groups=groups, tiled=True)

        after, before = walk_get(term, 4), walk_get(term, -4)
        place = walk // 2 // 4
        first = jnp.where(place == 0, term, jnp.where(place == 1, before, after))
        second = jnp.where(place == 0, after, jnp.where(place == 1, term, before))
        third = jnp.where(place == 0, before, jnp.where(place == 1, after, term))
        term = (first + second) + third
        term = term + walk_get(term, 2)

        mine, term = tie((jnp.sum(mine, axis=0), term))
        pair = lax.ppermute(mine[:2 * SLICE], ("walk", "par"), pair_perm)
        single = lax.ppermute(mine[2 * SLICE:], ("walk", "par"), single_perm)
        update = term + walk_get(term, 1)
        gram = jnp.where(
            par % 4 == 1,
            jnp.concatenate((single, pair), axis=0),
            jnp.concatenate((pair, single), axis=0),
        )
        return gram.T, update

    in_specs = (P("walk", "par"), P("walk"))
    out_specs = (P("walk", "par"), P("par"))
    return jax.shard_map(shards, mesh=mesh, in_specs=in_specs, out_specs=out_specs, check_vma=False)
```

```python
import functools

import numpy as np
import jax
import jax.numpy as jnp
from jax import lax
from jax.experimental import pallas as pl
from jax.experimental.pallas import tpu as pltpu
from jax.sharding import PartitionSpec as P

NZ = 12
NQ = 16
SLICE = 32

BLOCKS = ((0, 0), (1, 0), (2, 0), (-3, 0), (0, 1), (1, 1), (3, 0), (-3, 1))
EARLY = (0, 1, 2, 3, 4, 5)
LATE = (1, 2, 3, 6, 7)
NEARLY, NLATE, SHARE = 9, 3, 12

SHARES = (
    (
        ((2, 5), (5, 3), (4, 3), (3, 0), (0, 2), (4, 2), (3, 4), (1, 1), (5, 1), (6, 7), (7, 1), (6, 1)),
        ((2, 3), (1, 3), (0, 3), (3, 2), (2, 4), (2, 1), (0, 1), (4, 1), (3, 1), (3, 6), (7, 2), (2, 7)),
    ),
    (
        ((5, 1), (4, 1), (3, 4), (3, 1), (2, 0), (5, 3), (4, 3), (2, 2), (1, 2), (3, 6), (6, 2), (7, 2)),
        ((2, 4), (3, 0), (2, 3), (1, 3), (0, 3), (2, 5), (0, 2), (4, 2), (3, 2), (6, 7), (7, 1), (2, 7)),
    ),
)


def walker_block(walk, block):
    d, e = BLOCKS[block]
    return 2 * ((walk // 2 + d) % NZ) + (walk % 2 ^ e)


def place_of(index):
    par, slot = divmod(index, 3)
    return (slot + 2) % 3 if par % 4 == 1 else slot


def ring_distance(a, b, n):
    return min((a - b) % n, (b - a) % n)


def distance(source, target):
    (w0, p0), (w1, p1) = source, target
    x0, x1 = (p0 // 16) * 2 + w0 % 2, (p1 // 16) * 2 + w1 % 2
    return (
        ring_distance(w0 // 2, w1 // 2, NZ)
        + ring_distance(x0, x1, 4)
        + ring_distance(p0 // 2 % 8, p1 // 2 % 8, 8)
    )


def assign(walk, core, targets):
    cost = [[distance((walk, q * 2 + core), t) ** 2 for q in range(NQ)] for t in targets]
    pick = []
    for row in cost:
        pick.append(min((q for q in range(NQ) if q not in pick), key=lambda q: row[q]))
    better = True
    while better:
        better = False
        for a in range(NQ):
            for b in range(a):
                now = cost[a][pick[a]] + cost[b][pick[b]]
                if cost[a][pick[b]] + cost[b][pick[a]] < now:
                    pick[a], pick[b] = pick[b], pick[a]
                    better = True
    return pick


def held(block, core):
    return block ^ 1 if core and block in (2, 3, 6, 7) else block


def plan():
    early_table = np.zeros((2 * NZ, 2, 2, NEARLY, 2), np.int32)
    late_table = np.zeros((2 * NZ, 2, 2, NLATE, 2), np.int32)
    places = np.zeros((2 * NZ, 2, SHARE, 4), np.int32)
    pairs = [[], [], []]
    seen = set()
    for walk in range(2 * NZ):
        for core, share in enumerate(SHARES[walk % 2]):
            slices = []
            for n, (row, col) in enumerate(share):
                for k in range(4):
                    index = 4 * walker_block(walk, col) + k
                    target = (walker_block(walk, row), index // 3)
                    slices.append((n, k, place_of(index), target))
            for slot in range(3):
                chosen = [s for s in slices if s[2] == slot]
                if slot != 1:
                    picks = assign(walk, core, [s[3] for s in chosen])
                for (n, k, _, target), q in zip(chosen, picks, strict=True):
                    places[walk, core, n, k] = q * 3 + slot
                    source = walk * 2 * NQ + q * 2 + core
                    pairs[slot].append((source, target[0] * 2 * NQ + target[1]))
                    seen.add((target, slot))
            for n, (row, col) in enumerate(share):
                for mine in range(2):
                    at = [held(row, mine), held(col, mine)]
                    if n < NEARLY:
                        early_table[walk, mine, int(core != mine), n] = [EARLY.index(b) for b in at]
                    else:
                        late_table[walk, mine, int(core != mine), n - NEARLY] = [LATE.index(b) for b in at]
    assert len(seen) == NZ * 2 * 2 * NQ * 3
    assert sorted(pairs[0]) == sorted(pairs[1])
    tables = [t.reshape(4 * NZ, -1) for t in (early_table, late_table, places)]
    return np.concatenate(tables, axis=1), pairs[0], pairs[2]


def product_kernel(base, count, ready, shared, table, *refs):
    done, blocks, (keep, send) = refs[:ready], refs[ready:-3 - bool(shared)], refs[-3 - bool(shared):][:2]
    parts = refs[-1]
    depth = blocks[0].shape[1]
    if ready:
        parts[:done[0].shape[0]] = done[0][...]
    first = done[0].shape[0] if ready else 0
    for b, ref in enumerate(blocks):
        value = ref[...]
        high = value.astype(jnp.bfloat16)
        parts[first + b, :, :depth] = high
        parts[first + b, :, depth:] = (value - high.astype(jnp.float32)).astype(jnp.bfloat16)
    if shared:
        refs[-2][...] = parts[shared[0]:shared[1]]
    dims = (((1,), (1,)), ((), ()))

    def dot(left, right):
        return lax.dot_general(left, right, dims, preferred_element_type=jnp.float32)

    for half, out in ((1, send), (0, keep)):
        for n in range(count):
            at = base + (half * count + n) * 2
            row, col = table[at], table[at + 1]
            row_high, row_low = parts[row, :, :depth], parts[row, :, depth:]
            col_high, col_low = parts[col, :, :depth], parts[col, :, depth:]
            out[n] = dot(col_high, row_high) + (dot(col_high, row_low) + dot(col_low, row_high))


VMEM = pl.BlockSpec(memory_space=pltpu.VMEM)
SMEM = pl.BlockSpec(memory_space=pltpu.SMEM)


def products(table, base, count, blocks, cost, ready=(), shared=()):
    rows, depth = blocks[0].shape
    out = [jax.ShapeDtypeStruct((count, rows, rows), jnp.float32)] * 2
    if shared:
        out.append(jax.ShapeDtypeStruct((shared[1] - shared[0], rows, 2 * depth), jnp.bfloat16))
    total = len(blocks) + sum(r.shape[0] for r in ready)
    return pl.pallas_call(
        functools.partial(product_kernel, base, count, len(ready), shared),
        out_shape=out,
        in_specs=[SMEM] + [VMEM] * (len(ready) + len(blocks)),
        out_specs=[VMEM] * len(out),
        scratch_shapes=[pltpu.VMEM((total, rows, 2 * depth), jnp.bfloat16)],
        compiler_params=pltpu.CompilerParams(vmem_limit_bytes=32 * 2**20),
        cost_estimate=pl.CostEstimate(flops=cost, bytes_accessed=2**20, transcendentals=0),
    )(table, *ready, *blocks)


def join_kernel(table, *refs):
    *terms, out = refs
    at = 4 * SHARE
    for kept, got in (terms[:2], terms[2:]):
        for n in range(kept.shape[0]):
            tile = kept[n] + got[n]
            for k in range(4):
                out[table[at]] = tile[k * SLICE:(k + 1) * SLICE]
                at += 1


def join(table, *terms):
    return pl.pallas_call(
        join_kernel,
        out_shape=jax.ShapeDtypeStruct((3 * NQ, SLICE, terms[0].shape[2]), jnp.float32),
        in_specs=[SMEM] + [VMEM] * len(terms),
        out_specs=VMEM,
        compiler_params=pltpu.CompilerParams(vmem_limit_bytes=32 * 2**20),
    )(table, *terms)


def walk_perm(dz, flip):
    return [
        (((z + dz) % NZ) * 2 + (x ^ flip), z * 2 + x) for z in range(NZ) for x in range(2)
    ]


def mixed_perm(moves):
    return [
        (source * 2 * NQ + p, target * 2 * NQ + p)
        for p in range(2 * NQ)
        for source, target in walk_perm(*moves[p % 2])
    ]


def solution(mesh):
    tables, pair_perm, single_perm = plan()
    core_swap = [(p, p ^ 1) for p in range(2 * NQ)]
    groups = [[q * 2 + c for q in range(NQ)] for c in range(2)]

    def shards(jacobian, coeffs):
        walk, par = lax.axis_index("walk"), lax.axis_index("par")
        table = lax.dynamic_index_in_dim(
            jnp.asarray(tables), walk * 2 + par % 2, 0, keepdims=False
        )
        tie = lax.optimization_barrier

        def walk_get(value, dz, flip=0):
            return lax.ppermute(value, "walk", walk_perm(dz, flip))

        def mixed_get(value, *moves):
            return lax.ppermute(value, ("walk", "par"), mixed_perm(moves))

        far_a = mixed_get(jacobian, (2, 0), (-3, 0))
        far_b = mixed_get(jacobian, (-3, 0), (2, 0))
        up1 = walk_get(jacobian, 1)
        pair0 = walk_get(jacobian, 0, 1)
        pair1 = walk_get(up1, 0, 1)
        term = jnp.sum(coeffs[:, None] * jacobian, axis=0)
        far_a, pair0, term, table = tie((far_a, pair0, term + walk_get(term, 0, 1), table))
        far_b, pair1 = tie((far_b, pair1))
        late_a = mixed_get(far_a, (1, 0), (0, 1))
        late_b = mixed_get(far_b, (0, 1), (1, 0))

        keep, send, split = products(
            table, 0, NEARLY, (jacobian, up1, far_a, far_b, pair0, pair1), 2**28, shared=(1, 4)
        )
        early = (keep, lax.ppermute(send, "par", core_swap))
        keep, send = products(table, 4 * NEARLY, NLATE, (late_a, late_b), 2**35, ready=(split,))
        late = (keep, lax.ppermute(send, "par", core_swap))

        mine = join(table, *early, *late).reshape(NQ, 3 * SLICE, -1)
        mine, term = tie((mine, term))
        mine = lax.all_to_all(mine, "par", 0, 0, axis_index_groups=groups, tiled=True)

        after, before = walk_get(term, 4), walk_get(term, -4)
        place = walk // 2 // 4
        first = jnp.where(place == 0, term, jnp.where(place == 1, before, after))
        second = jnp.where(place == 0, after, jnp.where(place == 1, term, before))
        third = jnp.where(place == 0, before, jnp.where(place == 1, after, term))
        term = (first + second) + third
        update = (term + walk_get(term, 2)) + (walk_get(term, 1) + walk_get(term, -1))

        mine = jnp.sum(mine, axis=0)
        pair = lax.ppermute(mine[:2 * SLICE], ("walk", "par"), pair_perm)
        single = lax.ppermute(mine[2 * SLICE:], ("walk", "par"), single_perm)
        gram = jnp.where(
            par % 4 == 1,
            jnp.concatenate((single, pair), axis=0),
            jnp.concatenate((pair, single), axis=0),
        )
        return gram.T, update

    in_specs = (P("walk", "par"), P("walk"))
    out_specs = (P("walk", "par"), P("par"))
    return jax.shard_map(shards, mesh=mesh, in_specs=in_specs, out_specs=out_specs, check_vma=False)
```

```python
import functools

import numpy as np
import jax
import jax.numpy as jnp
from jax import lax
from jax.experimental import pallas as pl
from jax.experimental.pallas import tpu as pltpu
from jax.sharding import PartitionSpec as P

NZ = 12
NQ = 16
SLICE = 32

BLOCKS = ((0, 0), (1, 0), (2, 0), (-3, 0), (0, 1), (1, 1), (3, 0), (-3, 1))
EARLY = (0, 1, 2, 3, 4, 5)
LATE = (1, 2, 3, 6, 7)
NEARLY, NLATE, SHARE = 9, 3, 12

SHARES = (
    (
        ((2, 5), (5, 3), (4, 3), (3, 0), (0, 2), (4, 2), (3, 4), (1, 1), (5, 1), (6, 7), (7, 1), (6, 1)),
        ((2, 3), (1, 3), (0, 3), (3, 2), (2, 4), (2, 1), (0, 1), (4, 1), (3, 1), (3, 6), (7, 2), (2, 7)),
    ),
    (
        ((5, 1), (4, 1), (3, 4), (3, 1), (2, 0), (5, 3), (4, 3), (2, 2), (1, 2), (3, 6), (6, 2), (7, 2)),
        ((2, 4), (3, 0), (2, 3), (1, 3), (0, 3), (2, 5), (0, 2), (4, 2), (3, 2), (6, 7), (7, 1), (2, 7)),
    ),
)


def walker_block(walk, block):
    d, e = BLOCKS[block]
    return 2 * ((walk // 2 + d) % NZ) + (walk % 2 ^ e)


def place_of(index):
    par, slot = divmod(index, 3)
    return (slot + 2) % 3 if par % 4 == 1 else slot


def ring_distance(a, b, n):
    return min((a - b) % n, (b - a) % n)


def distance(source, target):
    (w0, p0), (w1, p1) = source, target
    x0, x1 = (p0 // 16) * 2 + w0 % 2, (p1 // 16) * 2 + w1 % 2
    return (
        ring_distance(w0 // 2, w1 // 2, NZ)
        + ring_distance(x0, x1, 4)
        + ring_distance(p0 // 2 % 8, p1 // 2 % 8, 8)
    )


def assign(walk, core, targets):
    cost = [[distance((walk, q * 2 + core), t) ** 2 for q in range(NQ)] for t in targets]
    pick = []
    for row in cost:
        pick.append(min((q for q in range(NQ) if q not in pick), key=lambda q: row[q]))
    better = True
    while better:
        better = False
        for a in range(NQ):
            for b in range(a):
                now = cost[a][pick[a]] + cost[b][pick[b]]
                if cost[a][pick[b]] + cost[b][pick[a]] < now:
                    pick[a], pick[b] = pick[b], pick[a]
                    better = True
    return pick


def held(block, core):
    return block ^ 1 if core and block in (2, 3, 6, 7) else block


def plan():
    early_table = np.zeros((2 * NZ, 2, 2, NEARLY, 2), np.int32)
    late_table = np.zeros((2 * NZ, 2, 2, NLATE, 2), np.int32)
    places = np.zeros((2 * NZ, 2, SHARE, 4), np.int32)
    pairs = [[], [], []]
    seen = set()
    for walk in range(2 * NZ):
        for core, share in enumerate(SHARES[walk % 2]):
            slices = []
            for n, (row, col) in enumerate(share):
                for k in range(4):
                    index = 4 * walker_block(walk, col) + k
                    target = (walker_block(walk, row), index // 3)
                    slices.append((n, k, place_of(index), target))
            for slot in range(3):
                chosen = [s for s in slices if s[2] == slot]
                if slot != 1:
                    picks = assign(walk, core, [s[3] for s in chosen])
                for (n, k, _, target), q in zip(chosen, picks, strict=True):
                    places[walk, core, n, k] = q * 3 + slot
                    source = walk * 2 * NQ + q * 2 + core
                    pairs[slot].append((source, target[0] * 2 * NQ + target[1]))
                    seen.add((target, slot))
            for n, (row, col) in enumerate(share):
                for mine in range(2):
                    at = [held(row, mine), held(col, mine)]
                    if n < NEARLY:
                        early_table[walk, mine, int(core != mine), n] = [EARLY.index(b) for b in at]
                    else:
                        late_table[walk, mine, int(core != mine), n - NEARLY] = [LATE.index(b) for b in at]
    assert len(seen) == NZ * 2 * 2 * NQ * 3
    assert sorted(pairs[0]) == sorted(pairs[1])
    tables = [t.reshape(4 * NZ, -1) for t in (early_table, late_table, places)]
    return np.concatenate(tables, axis=1), pairs[0], pairs[2]


def product_kernel(base, count, ready, shared, table, *refs):
    done, blocks, (keep, send) = refs[:ready], refs[ready:-3 - bool(shared)], refs[-3 - bool(shared):][:2]
    parts = refs[-1]
    depth = blocks[0].shape[1]
    if ready:
        parts[:done[0].shape[0]] = done[0][...]
    first = done[0].shape[0] if ready else 0
    for b, ref in enumerate(blocks):
        value = ref[...]
        high = value.astype(jnp.bfloat16)
        parts[first + b, :, :depth] = high
        parts[first + b, :, depth:] = (value - high.astype(jnp.float32)).astype(jnp.bfloat16)
    if shared:
        refs[-2][...] = parts[shared[0]:shared[1]]
    dims = (((1,), (1,)), ((), ()))

    def dot(left, right):
        return lax.dot_general(left, right, dims, preferred_element_type=jnp.float32)

    for half, out in ((1, send), (0, keep)):
        for n in range(count):
            at = base + (half * count + n) * 2
            row, col = table[at], table[at + 1]
            row_high, row_low = parts[row, :, :depth], parts[row, :, depth:]
            col_high, col_low = parts[col, :, :depth], parts[col, :, depth:]
            out[n] = dot(col_high, row_high) + (dot(col_high, row_low) + dot(col_low, row_high))


VMEM = pl.BlockSpec(memory_space=pltpu.VMEM)
SMEM = pl.BlockSpec(memory_space=pltpu.SMEM)


def products(table, base, count, blocks, cost, ready=(), shared=()):
    rows, depth = blocks[0].shape
    out = [jax.ShapeDtypeStruct((count, rows, rows), jnp.float32)] * 2
    if shared:
        out.append(jax.ShapeDtypeStruct((shared[1] - shared[0], rows, 2 * depth), jnp.bfloat16))
    total = len(blocks) + sum(r.shape[0] for r in ready)
    return pl.pallas_call(
        functools.partial(product_kernel, base, count, len(ready), shared),
        out_shape=out,
        in_specs=[SMEM] + [VMEM] * (len(ready) + len(blocks)),
        out_specs=[VMEM] * len(out),
        scratch_shapes=[pltpu.VMEM((total, rows, 2 * depth), jnp.bfloat16)],
        compiler_params=pltpu.CompilerParams(vmem_limit_bytes=32 * 2**20),
        cost_estimate=pl.CostEstimate(flops=cost, bytes_accessed=2**20, transcendentals=0),
    )(table, *ready, *blocks)


def join_kernel(table, *refs):
    *terms, out = refs
    at = 4 * SHARE
    for kept, got in (terms[:2], terms[2:]):
        for n in range(kept.shape[0]):
            tile = kept[n] + got[n]
            for k in range(4):
                out[table[at]] = tile[k * SLICE:(k + 1) * SLICE]
                at += 1


def join(table, *terms):
    return pl.pallas_call(
        join_kernel,
        out_shape=jax.ShapeDtypeStruct((3 * NQ, SLICE, terms[0].shape[2]), jnp.float32),
        in_specs=[SMEM] + [VMEM] * len(terms),
        out_specs=VMEM,
        compiler_params=pltpu.CompilerParams(vmem_limit_bytes=32 * 2**20),
    )(table, *terms)


def walk_perm(dz, flip):
    return [
        (((z + dz) % NZ) * 2 + (x ^ flip), z * 2 + x) for z in range(NZ) for x in range(2)
    ]


def mixed_perm(moves):
    return [
        (source * 2 * NQ + p, target * 2 * NQ + p)
        for p in range(2 * NQ)
        for source, target in walk_perm(*moves[p % 2])
    ]


def solution(mesh):
    tables, pair_perm, single_perm = plan()
    core_swap = [(p, p ^ 1) for p in range(2 * NQ)]
    groups = [[q * 2 + c for q in range(NQ)] for c in range(2)]

    def shards(jacobian, coeffs):
        walk, par = lax.axis_index("walk"), lax.axis_index("par")
        table = lax.dynamic_index_in_dim(
            jnp.asarray(tables), walk * 2 + par % 2, 0, keepdims=False
        )
        tie = lax.optimization_barrier

        def walk_get(value, dz, flip=0):
            return lax.ppermute(value, "walk", walk_perm(dz, flip))

        def mixed_get(value, *moves):
            return lax.ppermute(value, ("walk", "par"), mixed_perm(moves))

        far_a = mixed_get(jacobian, (2, 0), (-3, 0))
        far_b = mixed_get(jacobian, (-3, 0), (2, 0))
        up1 = walk_get(jacobian, 1)
        pair0 = walk_get(jacobian, 0, 1)
        pair1 = walk_get(up1, 0, 1)
        term = jnp.sum(coeffs[:, None] * jacobian, axis=0)
        far_a, term, table = tie((far_a, term + walk_get(term, 0, 1), table))
        late_a = mixed_get(far_a, (1, 0), (0, 1))
        late_b = mixed_get(far_b, (0, 1), (1, 0))

        keep, send, split = products(
            table, 0, NEARLY, (jacobian, up1, far_a, far_b, pair0, pair1), 2**28, shared=(1, 4)
        )
        early = (keep, lax.ppermute(send, "par", core_swap))
        keep, send = products(table, 4 * NEARLY, NLATE, (late_a, late_b), 2**35, ready=(split,))
        late = (keep, lax.ppermute(send, "par", core_swap))

        mine = join(table, *early, *late).reshape(NQ, 3 * SLICE, -1)
        mine, term = tie((mine, term))
        mine = lax.all_to_all(mine, "par", 0, 0, axis_index_groups=groups, tiled=True)

        after, before = walk_get(term, 4), walk_get(term, -4)
        place = walk // 2 // 4
        first = jnp.where(place == 0, term, jnp.where(place == 1, before, after))
        second = jnp.where(place == 0, after, jnp.where(place == 1, term, before))
        third = jnp.where(place == 0, before, jnp.where(place == 1, after, term))
        term = (first + second) + third
        update = (term + walk_get(term, 2)) + (walk_get(term, 1) + walk_get(term, -1))

        mine = jnp.sum(mine, axis=0)
        pair = lax.ppermute(mine[:2 * SLICE], ("walk", "par"), pair_perm)
        single = lax.ppermute(mine[2 * SLICE:], ("walk", "par"), single_perm)
        gram = jnp.where(
            par % 4 == 1,
            jnp.concatenate((single, pair), axis=0),
            jnp.concatenate((pair, single), axis=0),
        )
        return gram.T, update

    in_specs = (P("walk", "par"), P("walk"))
    out_specs = (P("walk", "par"), P("par"))
    return jax.shard_map(shards, mesh=mesh, in_specs=in_specs, out_specs=out_specs, check_vma=False)
```

```python
import functools

import numpy as np
import jax
import jax.numpy as jnp
from jax import lax
from jax.experimental import pallas as pl
from jax.experimental.pallas import tpu as pltpu
from jax.sharding import PartitionSpec as P

NZ = 12
NQ = 16
SLICE = 32

BLOCKS = ((0, 0), (1, 0), (2, 0), (-3, 0), (0, 1), (1, 1), (3, 0), (-3, 1))
EARLY = (0, 1, 2, 3, 4, 5)
LATE = (1, 2, 3, 6, 7)
NEARLY, NLATE, SHARE = 9, 3, 12

SHARES = (
    (
        ((2, 5), (5, 3), (4, 3), (3, 0), (0, 2), (4, 2), (3, 4), (1, 1), (5, 1), (6, 7), (7, 1), (6, 1)),
        ((2, 3), (1, 3), (0, 3), (3, 2), (2, 4), (2, 1), (0, 1), (4, 1), (3, 1), (3, 6), (7, 2), (2, 7)),
    ),
    (
        ((5, 1), (4, 1), (3, 4), (3, 1), (2, 0), (5, 3), (4, 3), (2, 2), (1, 2), (3, 6), (6, 2), (7, 2)),
        ((2, 4), (3, 0), (2, 3), (1, 3), (0, 3), (2, 5), (0, 2), (4, 2), (3, 2), (6, 7), (7, 1), (2, 7)),
    ),
)


def walker_block(walk, block):
    d, e = BLOCKS[block]
    return 2 * ((walk // 2 + d) % NZ) + (walk % 2 ^ e)


def place_of(index):
    par, slot = divmod(index, 3)
    return (slot + 2) % 3 if par % 4 == 1 else slot


def ring_distance(a, b, n):
    return min((a - b) % n, (b - a) % n)


def distance(source, target):
    (w0, p0), (w1, p1) = source, target
    x0, x1 = (p0 // 16) * 2 + w0 % 2, (p1 // 16) * 2 + w1 % 2
    return (
        ring_distance(w0 // 2, w1 // 2, NZ)
        + ring_distance(x0, x1, 4)
        + ring_distance(p0 // 2 % 8, p1 // 2 % 8, 8)
    )


def assign(walk, core, targets):
    cost = [[distance((walk, q * 2 + core), t) ** 2 for q in range(NQ)] for t in targets]
    pick = []
    for row in cost:
        pick.append(min((q for q in range(NQ) if q not in pick), key=lambda q: row[q]))
    better = True
    while better:
        better = False
        for a in range(NQ):
            for b in range(a):
                now = cost[a][pick[a]] + cost[b][pick[b]]
                if cost[a][pick[b]] + cost[b][pick[a]] < now:
                    pick[a], pick[b] = pick[b], pick[a]
                    better = True
    return pick


def held(block, core):
    return block ^ 1 if core and block in (2, 3, 6, 7) else block


def plan():
    early_table = np.zeros((2 * NZ, 2, 2, NEARLY, 2), np.int32)
    late_table = np.zeros((2 * NZ, 2, 2, NLATE, 2), np.int32)
    places = np.zeros((2 * NZ, 2, SHARE, 4), np.int32)
    pairs = [[], [], []]
    seen = set()
    for walk in range(2 * NZ):
        for core, share in enumerate(SHARES[walk % 2]):
            slices = []
            for n, (row, col) in enumerate(share):
                for k in range(4):
                    index = 4 * walker_block(walk, col) + k
                    target = (walker_block(walk, row), index // 3)
                    slices.append((n, k, place_of(index), target))
            for slot in range(3):
                chosen = [s for s in slices if s[2] == slot]
                if slot != 1:
                    picks = assign(walk, core, [s[3] for s in chosen])
                for (n, k, _, target), q in zip(chosen, picks, strict=True):
                    places[walk, core, n, k] = q * 3 + slot
                    source = walk * 2 * NQ + q * 2 + core
                    pairs[slot].append((source, target[0] * 2 * NQ + target[1]))
                    seen.add((target, slot))
            for n, (row, col) in enumerate(share):
                for mine in range(2):
                    at = [held(row, mine), held(col, mine)]
                    if n < NEARLY:
                        early_table[walk, mine, int(core != mine), n] = [EARLY.index(b) for b in at]
                    else:
                        late_table[walk, mine, int(core != mine), n - NEARLY] = [LATE.index(b) for b in at]
    assert len(seen) == NZ * 2 * 2 * NQ * 3
    assert sorted(pairs[0]) == sorted(pairs[1])
    tables = [t.reshape(4 * NZ, -1) for t in (early_table, late_table, places)]
    return np.concatenate(tables, axis=1), pairs[0], pairs[2]


def product_kernel(base, count, ready, shared, table, *refs):
    done, blocks, (keep, send) = refs[:ready], refs[ready:-3 - bool(shared)], refs[-3 - bool(shared):][:2]
    parts = refs[-1]
    depth = blocks[0].shape[1]
    if ready:
        parts[:done[0].shape[0]] = done[0][...]
    first = done[0].shape[0] if ready else 0
    for b, ref in enumerate(blocks):
        value = ref[...]
        high = value.astype(jnp.bfloat16)
        parts[first + b, :, :depth] = high
        parts[first + b, :, depth:] = (value - high.astype(jnp.float32)).astype(jnp.bfloat16)
    if shared:
        refs[-2][...] = parts[shared[0]:shared[1]]
    dims = (((1,), (1,)), ((), ()))

    def dot(left, right):
        return lax.dot_general(left, right, dims, preferred_element_type=jnp.float32)

    for half, out in ((1, send), (0, keep)):
        for n in range(count):
            at = base + (half * count + n) * 2
            row, col = table[at], table[at + 1]
            row_high, row_low = parts[row, :, :depth], parts[row, :, depth:]
            col_high, col_low = parts[col, :, :depth], parts[col, :, depth:]
            out[n] = dot(col_high, row_high) + (dot(col_high, row_low) + dot(col_low, row_high))


VMEM = pl.BlockSpec(memory_space=pltpu.VMEM)
SMEM = pl.BlockSpec(memory_space=pltpu.SMEM)


def products(table, base, count, blocks, cost, ready=(), shared=()):
    rows, depth = blocks[0].shape
    out = [jax.ShapeDtypeStruct((count, rows, rows), jnp.float32)] * 2
    if shared:
        out.append(jax.ShapeDtypeStruct((shared[1] - shared[0], rows, 2 * depth), jnp.bfloat16))
    total = len(blocks) + sum(r.shape[0] for r in ready)
    return pl.pallas_call(
        functools.partial(product_kernel, base, count, len(ready), shared),
        out_shape=out,
        in_specs=[SMEM] + [VMEM] * (len(ready) + len(blocks)),
        out_specs=[VMEM] * len(out),
        scratch_shapes=[pltpu.VMEM((total, rows, 2 * depth), jnp.bfloat16)],
        compiler_params=pltpu.CompilerParams(vmem_limit_bytes=32 * 2**20),
        cost_estimate=pl.CostEstimate(flops=cost, bytes_accessed=2**20, transcendentals=0),
    )(table, *ready, *blocks)


def join_kernel(table, *refs):
    *terms, out = refs
    at = 4 * SHARE
    for kept, got in (terms[:2], terms[2:]):
        for n in range(kept.shape[0]):
            tile = kept[n] + got[n]
            for k in range(4):
                out[table[at]] = tile[k * SLICE:(k + 1) * SLICE]
                at += 1


def join(table, *terms):
    return pl.pallas_call(
        join_kernel,
        out_shape=jax.ShapeDtypeStruct((3 * NQ, SLICE, terms[0].shape[2]), jnp.float32),
        in_specs=[SMEM] + [VMEM] * len(terms),
        out_specs=VMEM,
        compiler_params=pltpu.CompilerParams(vmem_limit_bytes=32 * 2**20),
    )(table, *terms)


def walk_perm(dz, flip):
    return [
        (((z + dz) % NZ) * 2 + (x ^ flip), z * 2 + x) for z in range(NZ) for x in range(2)
    ]


def mixed_perm(moves):
    return [
        (source * 2 * NQ + p, target * 2 * NQ + p)
        for p in range(2 * NQ)
        for source, target in walk_perm(*moves[p % 2])
    ]


def solution(mesh):
    tables, pair_perm, single_perm = plan()
    core_swap = [(p, p ^ 1) for p in range(2 * NQ)]
    groups = [[q * 2 + c for q in range(NQ)] for c in range(2)]

    def shards(jacobian, coeffs):
        walk, par = lax.axis_index("walk"), lax.axis_index("par")
        table = lax.dynamic_index_in_dim(
            jnp.asarray(tables), walk * 2 + par % 2, 0, keepdims=False
        )
        tie = lax.optimization_barrier

        def walk_get(value, dz, flip=0):
            return lax.ppermute(value, "walk", walk_perm(dz, flip))

        def mixed_get(value, *moves):
            return lax.ppermute(value, ("walk", "par"), mixed_perm(moves))

        far_a = mixed_get(jacobian, (2, 0), (-3, 0))
        far_b = mixed_get(jacobian, (-3, 0), (2, 0))
        up1 = walk_get(jacobian, 1)
        pair0 = walk_get(jacobian, 0, 1)
        pair1 = walk_get(up1, 0, 1)
        term = jnp.sum(coeffs[:, None] * jacobian, axis=0)
        far_b, term, table = tie((far_b, term + walk_get(term, 0, 1), table))
        late_a = mixed_get(far_a, (1, 0), (0, 1))
        late_b = mixed_get(far_b, (0, 1), (1, 0))

        keep, send, split = products(
            table, 0, NEARLY, (jacobian, up1, far_a, far_b, pair0, pair1), 2**28, shared=(1, 4)
        )
        early = (keep, lax.ppermute(send, "par", core_swap))
        keep, send = products(table, 4 * NEARLY, NLATE, (late_a, late_b), 2**35, ready=(split,))
        late = (keep, lax.ppermute(send, "par", core_swap))

        mine = join(table, *early, *late).reshape(NQ, 3 * SLICE, -1)
        mine, term = tie((mine, term))
        mine = lax.all_to_all(mine, "par", 0, 0, axis_index_groups=groups, tiled=True)

        after, before = walk_get(term, 4), walk_get(term, -4)
        place = walk // 2 // 4
        first = jnp.where(place == 0, term, jnp.where(place == 1, before, after))
        second = jnp.where(place == 0, after, jnp.where(place == 1, term, before))
        third = jnp.where(place == 0, before, jnp.where(place == 1, after, term))
        term = (first + second) + third
        update = (term + walk_get(term, 2)) + (walk_get(term, 1) + walk_get(term, -1))

        mine = jnp.sum(mine, axis=0)
        pair = lax.ppermute(mine[:2 * SLICE], ("walk", "par"), pair_perm)
        single = lax.ppermute(mine[2 * SLICE:], ("walk", "par"), single_perm)
        gram = jnp.where(
            par % 4 == 1,
            jnp.concatenate((single, pair), axis=0),
            jnp.concatenate((pair, single), axis=0),
        )
        return gram.T, update

    in_specs = (P("walk", "par"), P("walk"))
    out_specs = (P("walk", "par"), P("par"))
    return jax.shard_map(shards, mesh=mesh, in_specs=in_specs, out_specs=out_specs, check_vma=False)
```
